32 devices in a mesh: chan: 8 (over z, core), tm: 4 (over y, x).
Axes of the slice: x: 2, y: 2, z: 4, core: 2. Of those that a mesh axis runs over, the one named last changes fastest.
Arguments:
- traces: float32 [256, 65536], P('chan', 'tm'), may hold values from -8 to 8
- live_channel: int32 [256], P('chan'), may hold values 0 or 1
- valid_segment: int32 [256, 256], P('chan', 'tm'), may hold values 0 or 1
Outputs:
- correlation: float32 [256, 256, 256], P('chan', 'tm')
The draws below stay inside these ranges and needn't reach their ends.
All inputs are finite; a program needn't handle non-finite values. No bound on the sum of `live_channel` or of `valid_segment` on one device may be relied on, other than what follows from the above.
Results may differ from the reference program's by a relative error of at most 0.003.
Values may be sent and summed in bfloat16 or wider, within the bound.
A program may use at most 192 MiB of HBM per device.

```python
import jax
import jax.numpy as jnp
from jax import lax

SEG_LEN = 256
BINS = 128
HALF_WIN = 64
SMOOTH = 4
CHANNELS = 256
SEGMENTS = 256
SAMPLES = 65536


def with_ends(result, own_key, low, high):
    extent = result.shape
    index_at = [jax.random.randint(jax.random.fold_in(own_key, axis), (), 0, extent[axis]) for axis in range(len(extent))]
    result = result.at[tuple(index_at)].set(low)
    longest = extent.index(max(extent))
    index_at[longest] = (index_at[longest] + 1) % extent[longest]
    return result.at[tuple(index_at)].set(high)


def shard_levels(own_key, dims, shards, smallest, largest):
    def one(dim, blocks):
        heights = jax.random.uniform(jax.random.fold_in(jax.random.fold_in(own_key, 6), dim), (blocks,), jnp.float32, smallest / len(shards), largest / len(shards))
        return jnp.repeat(jnp.exp(heights), dims[dim] // blocks).reshape((-1,) + (1,) * (len(dims) - dim - 1))

    loudness = one(*shards[0])
    for cut in shards[1:]:
        loudness = loudness * one(*cut)
    return loudness


def bell_draw(rng, shape, scale, reach, pieces=(), kind=jnp.bfloat16):
    values = jax.random.normal(rng, shape, jnp.float32) * scale
    if len(pieces) > 0:
        values = shard_levels(rng, shape, pieces, -0.22, 0.18) * values
    return jnp.clip(values, min=-reach, max=reach).astype(kind)


def setup_inputs(seed: int = 0) -> dict:
    seeds = jax.random.split(jax.random.key(seed), 4)
    return {
        "traces": bell_draw(seeds[0], (CHANNELS, SAMPLES), 1.0, 8.0, ((0, 8), (1, 4)), jnp.float32),
        "live_channel": with_ends((jax.random.randint(seeds[1], (CHANNELS,), 0, 16) < 15).astype(jnp.int32), jax.random.fold_in(seeds[1], 1), 0, 1),
        "valid_segment": with_ends((jax.random.randint(seeds[2], (CHANNELS, SEGMENTS), 0, 8) < 7).astype(jnp.int32), jax.random.fold_in(seeds[2], 1), 0, 1),
    }


def make_tables():
    length = SEG_LEN
    times_col = jnp.arange(length, dtype=jnp.int32)[:, None]
    freq_row = jnp.arange(BINS, dtype=jnp.int32)[None, :]
    phase = 2.0 * jnp.pi / length * (times_col * freq_row % length).astype(jnp.float32)
    forward_table = jnp.concatenate([jnp.cos(phase), -jnp.sin(phase)], axis=1)
    freq_col = jnp.arange(BINS, dtype=jnp.int32)[:, None]
    lag_row = jnp.arange(length, dtype=jnp.int32)[None, :] - BINS
    back_phase = 2.0 * jnp.pi / length * (freq_col * lag_row % length).astype(jnp.float32)
    inverse_table = jnp.concatenate([jnp.cos(back_phase), -jnp.sin(back_phase)], axis=0)
    bin_a = jnp.arange(BINS, dtype=jnp.int32)[:, None]
    bin_b = jnp.arange(BINS, dtype=jnp.int32)[None, :]
    smooth_table = (jnp.abs(bin_a - bin_b) <= SMOOTH).astype(jnp.float32) / (2.0 * SMOOTH + 1.0)
    bandpass = (jnp.arange(BINS, dtype=jnp.int32) > 0).astype(jnp.float32)
    return (forward_table, inverse_table, smooth_table, bandpass)

def reference(traces, live_channel, valid_segment):
    forward_table, inverse_table, smooth_table, bandpass = make_tables()
    highest = lax.Precision.HIGHEST
    padded = jnp.pad(jnp.abs(traces), ((0, 0), (HALF_WIN, HALF_WIN)))
    window_sum = lax.reduce_window(padded, jnp.zeros((), padded.dtype), lax.add, (1, 2 * HALF_WIN + 1), (1, 1), 'VALID')
    abs_level = window_sum / (2.0 * HALF_WIN + 1.0)
    normed = traces / (abs_level + 1e-05)
    segments = normed.reshape(CHANNELS, SEGMENTS, SEG_LEN)
    spectrum = jnp.dot(segments, forward_table, precision=highest, preferred_element_type=jnp.float32)
    spectrum = spectrum.reshape(CHANNELS, SEGMENTS, 2, BINS)
    spectral_power = spectrum[:, :, 0] ** 2 + spectrum[:, :, 1] ** 2
    smoothed = jnp.dot(spectral_power, smooth_table, precision=highest, preferred_element_type=jnp.float32)
    mean_power = lax.optimization_barrier(jnp.mean(spectral_power, axis=-1, keepdims=True))
    seg_mask = (live_channel[:, None] * valid_segment).astype(jnp.bfloat16)
    whiten_scale = bandpass * seg_mask.astype(jnp.float32)[:, :, None] / jnp.sqrt(smoothed + 0.1 * mean_power + 1e-06)
    whitened = (spectrum * whiten_scale[:, :, None, :]).astype(jnp.bfloat16)
    pair_count = jnp.dot(seg_mask, seg_mask.T, preferred_element_type=jnp.float32)
    local_white = whitened.astype(jnp.float32)
    turned = jnp.stack([local_white[:, :, 1], -local_white[:, :, 0]], axis=2)
    cross_real = jnp.einsum('iscf,jscf->ijf', local_white, local_white, precision=highest)
    cross_imag = jnp.einsum('iscf,jscf->ijf', local_white, turned, precision=highest)
    cross = jnp.stack([cross_real, cross_imag], axis=2).reshape(CHANNELS, CHANNELS, 2 * BINS)
    lagged = jnp.dot(cross, inverse_table, precision=highest, preferred_element_type=jnp.float32)
    return lagged * (2.0 / jnp.maximum(pair_count, 1.0))[:, :, None]
```

```python
import functools

import jax
import jax.numpy as jnp
import numpy as np
from jax import lax
from jax.experimental import pallas as pl
from jax.experimental.pallas import tpu as pltpu
from jax.sharding import PartitionSpec as P

SEG_LEN = 256
BINS = 128
HALF_WIN = 64
SMOOTH = 4
ROWS = 2 * BINS
LANES = 128
SUB = 16
CHAN_ROWS = 32
SEGS = 64
PER_LANE = LANES // CHAN_ROWS
MESH = pl.DeviceIdType.MESH


def split_table(table):
    high = table.astype(jnp.bfloat16)
    low = (table - high.astype(np.float32)).astype(jnp.bfloat16)
    return high, low


def make_tables():
    row_bin = np.arange(ROWS) // 2
    row_imag = np.arange(ROWS) % 2 == 1
    time = np.arange(SEG_LEN)
    phase = 2.0 * np.pi / SEG_LEN * (row_bin[:, None] * time[None, :] % SEG_LEN)
    forward = np.where(row_imag[:, None], -np.sin(phase), np.cos(phase)).astype(np.float32)
    lag = np.arange(SEG_LEN) - BINS
    back = 2.0 * np.pi / SEG_LEN * (row_bin[:, None] * lag[None, :] % SEG_LEN)
    inverse = np.where(row_imag[:, None], -np.sin(back), np.cos(back))
    inverse = (inverse * (row_bin > 0)[:, None]).astype(np.float32)
    smooth = np.abs(row_bin[:, None] - row_bin[None, :]) <= SMOOTH
    sample_in = np.arange(2 * SEG_LEN)[:, None] - SEG_LEN // 2
    sample_out = np.arange(SEG_LEN)[None, :]
    box = np.abs(sample_in - sample_out) <= HALF_WIN
    return (
        split_table(forward),
        split_table(inverse),
        smooth.astype(jnp.bfloat16),
        box.astype(jnp.bfloat16),
    )


def halves(value):
    high = value.astype(jnp.bfloat16)
    return high, (value - high.astype(jnp.float32)).astype(jnp.bfloat16)


def mm(a, b, dims=((1,), (0,))):
    return lax.dot_general(a, b, (dims, ((), ())), preferred_element_type=jnp.float32)


NT = ((1,), (1,))
TN = ((0,), (0,))


def spread_kernel(
    n_chan, n_tm,
    x_hbm, mask_ref, box_ref, fwd_hi, fwd_lo, smooth_ref,
    out_hbm,
    xpad, turned, send1, recv1, pair, cross, send2,
    halo_send, halo_recv, local_sem, send1_sem, recv1_sem, send2_sem, recv2_sem,
):
    n = n_chan * n_tm
    span = SEGS * SEG_LEN
    chunk = ROWS // n
    chan, tm = lax.axis_index("chan"), lax.axis_index("tm")
    me = chan * n_tm + tm

    def device(index):
        return {"chan": index // n_tm, "tm": lax.rem(index, n_tm)}

    fill = pltpu.make_async_copy(x_hbm, xpad.at[:, pl.ds(LANES, span)], local_sem.at[0])
    fill.start()

    barrier = pltpu.get_barrier_semaphore()

    def greet(k, _):
        pl.semaphore_signal(
            barrier, inc=1, device_id=device(lax.rem(me + k, n)), device_id_type=MESH
        )
        return 0

    lax.fori_loop(1, n, greet, 0)
    pl.semaphore_wait(barrier, n - 1)

    to_left = pltpu.make_async_remote_copy(
        src_ref=x_hbm.at[:, pl.ds(0, LANES)],
        dst_ref=xpad.at[:, pl.ds(LANES + span, LANES)],
        send_sem=halo_send.at[0], recv_sem=halo_recv.at[0],
        device_id={"chan": chan, "tm": jnp.maximum(tm - 1, 0)}, device_id_type=MESH,
    )
    to_right = pltpu.make_async_remote_copy(
        src_ref=x_hbm.at[:, pl.ds(span - LANES, LANES)],
        dst_ref=xpad.at[:, pl.ds(0, LANES)],
        send_sem=halo_send.at[1], recv_sem=halo_recv.at[1],
        device_id={"chan": chan, "tm": jnp.minimum(tm + 1, n_tm - 1)}, device_id_type=MESH,
    )
    has_left, has_right = tm > 0, tm < n_tm - 1

    @pl.when(has_left)
    def _():
        to_left.start()

    @pl.when(has_right)
    def _():
        to_right.start()

    @pl.when(jnp.logical_not(has_left))
    def _():
        xpad[:, 0:LANES] = jnp.zeros((CHAN_ROWS, LANES), jnp.float32)

    @pl.when(jnp.logical_not(has_right))
    def _():
        xpad[:, LANES + span : 2 * LANES + span] = jnp.zeros((CHAN_ROWS, LANES), jnp.float32)

    row = lax.broadcasted_iota(jnp.int32, (ROWS, 2 * LANES), 0)

    def whiten(m):
        window = jnp.concatenate(
            [
                xpad[:, pl.ds(pl.multiple_of(m * 8 * SEG_LEN + i * SEG_LEN, LANES), 2 * SEG_LEN)]
                for i in range(8)
            ],
            axis=0,
        )
        high, low = halves(jnp.abs(window))
        level = (mm(high, box_ref[...]) + mm(low, box_ref[...])) * (1.0 / (2 * HALF_WIN + 1))
        normed = window[:, SEG_LEN // 2 : SEG_LEN // 2 + SEG_LEN] / (level + 1e-5)
        high, low = halves(normed)
        spectrum = (
            mm(fwd_hi[...], high, NT) + mm(fwd_hi[...], low, NT) + mm(fwd_lo[...], high, NT)
        )
        power = spectrum * spectrum
        high, low = halves(power)
        smoothed = (mm(smooth_ref[...], high) + mm(smooth_ref[...], low)) * (
            1.0 / (2 * SMOOTH + 1)
        )
        mean_power = jnp.sum(power, axis=0, keepdims=True) * (1.0 / BINS)
        mask = jnp.concatenate(
            [mask_ref[pl.ds(2 * m, 1), :], mask_ref[pl.ds(2 * m + 1, 1), :]], axis=1
        )
        whitened = spectrum * (mask * lax.rsqrt(smoothed + (0.1 * mean_power + 1e-6)))
        whitened = jnp.where(row == 0, mask, jnp.where(row == 1, 0.0, whitened))
        for u in range(2):
            turned[pl.ds(pl.multiple_of((2 * m + u) * ROWS, ROWS), ROWS), :] = whitened[
                :, u * LANES : (u + 1) * LANES
            ]

    fill.wait()

    def inner(m, _):
        whiten(m)
        return 0

    last = SEGS // 8 - 1
    lax.fori_loop(1, last, inner, 0)

    @pl.when(has_left)
    def _():
        to_left.wait_send()
        to_right.wait_recv()

    @pl.when(has_right)
    def _():
        to_right.wait_send()
        to_left.wait_recv()

    def outer(m, _):
        whiten(m * last)
        return 0

    lax.fori_loop(0, 2, outer, 0)

    def turn(step, _):
        for i in range(8):
            r = step * 8 + i
            send1[r] = turned[pl.ds(r, SUB, stride=ROWS), :].astype(jnp.bfloat16)
        return 0

    lax.fori_loop(0, ROWS // 8, turn, 0)

    def exchange(source, target, send_sem, recv_sem, local):
        def part(index):
            return source.at[pl.ds(index * chunk, chunk)]

        def out_copy(to):
            return pltpu.make_async_remote_copy(
                src_ref=part(to), dst_ref=target.at[pl.ds(me * chunk, chunk)],
                send_sem=send_sem.at[to], recv_sem=recv_sem.at[me],
                device_id=device(to), device_id_type=MESH,
            )

        def in_copy(frm):
            return pltpu.make_async_remote_copy(
                src_ref=part(frm), dst_ref=target.at[pl.ds(frm * chunk, chunk)],
                send_sem=send_sem.at[frm], recv_sem=recv_sem.at[frm],
                device_id=device(frm), device_id_type=MESH,
            )

        own = pltpu.make_async_copy(part(me), target.at[pl.ds(me * chunk, chunk)], local)

        def start(k, _):
            out_copy(lax.rem(me + k, n)).start()
            return 0

        def arrive(k, _):
            in_copy(lax.rem(me + n - k, n)).wait_recv()
            return 0

        def leave(k, _):
            out_copy(lax.rem(me + k, n)).wait_send()
            return 0

        lax.fori_loop(1, n, start, 0)
        own.start()
        own.wait()
        lax.fori_loop(1, n, arrive, 0)
        return lambda: lax.fori_loop(1, n, leave, 0)

    left1 = exchange(send1, recv1, send1_sem, recv1_sem, local_sem.at[1])

    lane = lax.broadcasted_iota(jnp.int32, (SUB, LANES), 1)
    low_half = lane < LANES // 2
    even = lax.rem(lane // CHAN_ROWS, 2) == 0
    n_all = n_chan * CHAN_ROWS
    half_k = n_tm * SEGS

    def swap(first, second, distance, keep):
        return (
            jnp.where(keep, first, pltpu.roll(second, distance, 1)),
            jnp.where(keep, pltpu.roll(first, LANES - distance, 1), second),
        )

    def one_bin(f, _):
        for c in range(2):
            for b in range(n_tm):
                for g in range(n_chan // PER_LANE):
                    tiles = [
                        recv1[((g * PER_LANE + i) * n_tm + b) * chunk + 2 * f + c].astype(
                            jnp.float32
                        )
                        for i in range(PER_LANE)
                    ]
                    p0, p2 = swap(tiles[0], tiles[2], 64, low_half)
                    p1, p3 = swap(tiles[1], tiles[3], 64, low_half)
                    u0, u1 = swap(p0, p1, 32, even)
                    u2, u3 = swap(p2, p3, 32, even)
                    for q, value in enumerate((u0, u1, u2, u3)):
                        at = b * SEGS + q * SUB
                        pair[c * half_k + at : c * half_k + at + SUB, g * LANES : (g + 1) * LANES] = (
                            value.astype(jnp.bfloat16)
                        )
                        other = (1 - c) * half_k + at
                        pair[other : other + SUB, n_all + g * LANES : n_all + (g + 1) * LANES] = (
                            value if c == 1 else -value
                        ).astype(jnp.bfloat16)
        cross[...] = mm(pair[:, :n_all], pair[...], TN)
        counts = jnp.logical_and(me == 0, f == 0)
        for a in range(n_chan):
            for p in range(n_tm // 2):
                tops = []
                for c in range(2):
                    at = c * n_all + p * LANES
                    top = cross[a * CHAN_ROWS : a * CHAN_ROWS + SUB, at : at + LANES]
                    bottom = cross[a * CHAN_ROWS + SUB : (a + 1) * CHAN_ROWS, at : at + LANES]
                    tops.append(swap(top, bottom, 64, low_half))
                for i in range(2):
                    dest = (a * n_tm + 2 * p + i) * chunk + 2 * f
                    real = tops[0][i].astype(jnp.bfloat16)
                    rest = tops[0][i] - real.astype(jnp.float32)
                    send2[dest] = real
                    send2[dest + 1] = jnp.where(counts, rest, tops[1][i]).astype(jnp.bfloat16)
        return 0

    lax.fori_loop(0, chunk // 2, one_bin, 0)
    left2 = exchange(send2, out_hbm, send2_sem, recv2_sem, local_sem.at[2])
    left1()
    left2()


def lag_kernel(steps, cross_ref, inv_hi, inv_lo, out_ref, rows):
    step = pl.program_id(0)

    @pl.when(step == 0)
    def _():
        count = cross_ref[0].astype(jnp.float32) + cross_ref[1].astype(jnp.float32)
        scale = 2.0 / jnp.maximum(count, 1.0)

        def turn(block, _):
            for i in range(8):
                r = block * 8 + i
                rows[pl.ds(r, SUB, stride=ROWS), :] = cross_ref[r].astype(jnp.float32) * scale
            return 0

        lax.fori_loop(0, ROWS // 8, turn, 0)

    for i in range(SUB // steps):
        at = pl.multiple_of((step * (SUB // steps) + i) * ROWS, ROWS)
        high, low = halves(rows[pl.ds(at, ROWS), :])
        lagged = mm(high, inv_hi[...], TN) + mm(low, inv_hi[...], TN) + mm(high, inv_lo[...], TN)
        out_ref[0, i] = lagged[: LANES // 2]
        out_ref[1, i] = lagged[LANES // 2 :]


def body(n_chan, n_tm, traces, live_channel, valid_segment):
    (fwd_hi, fwd_lo), (inv_hi, inv_lo), smooth, box = make_tables()
    n = n_chan * n_tm
    n_all = n_chan * CHAN_ROWS
    span = traces.shape[1]
    mask = (live_channel[:, None] * valid_segment).astype(jnp.float32)
    mask = mask.T.reshape(SUB, LANES)
    vmem = pl.BlockSpec(memory_space=pltpu.VMEM)
    hbm = pl.BlockSpec(memory_space=pl.ANY)
    dma = pltpu.SemaphoreType.DMA
    tiles = (ROWS, SUB, LANES)
    crossed = pl.pallas_call(
        functools.partial(spread_kernel, n_chan, n_tm),
        out_shape=jax.ShapeDtypeStruct(tiles, jnp.bfloat16),
        in_specs=[hbm] + [vmem] * 5,
        out_specs=hbm,
        scratch_shapes=[
            pltpu.VMEM((CHAN_ROWS, span + 2 * LANES), jnp.float32),
            pltpu.VMEM((SUB * ROWS, LANES), jnp.float32),
            pltpu.VMEM(tiles, jnp.bfloat16),
            pltpu.VMEM(tiles, jnp.bfloat16),
            pltpu.VMEM((2 * n_tm * SEGS, 2 * n_all), jnp.bfloat16),
            pltpu.VMEM((n_all, 2 * n_all), jnp.float32),
            pltpu.VMEM(tiles, jnp.bfloat16),
            dma((2,)), dma((2,)), dma((3,)), dma((n,)), dma((n,)), dma((n,)), dma((n,)),
        ],
        compiler_params=pltpu.CompilerParams(
            collective_id=0, has_side_effects=True, vmem_limit_bytes=40 * 1024 * 1024
        ),
        name="spread",
    )(traces, mask, box, fwd_hi, fwd_lo, smooth)
    steps = 4
    whole = pl.BlockSpec((ROWS, SEG_LEN), lambda i: (0, 0))
    lagged = pl.pallas_call(
        functools.partial(lag_kernel, steps),
        out_shape=jax.ShapeDtypeStruct((2, SUB, LANES // 2, SEG_LEN), jnp.float32),
        grid=(steps,),
        in_specs=[pl.BlockSpec(tiles, lambda i: (0, 0, 0)), whole, whole],
        out_specs=pl.BlockSpec((2, SUB // steps, LANES // 2, SEG_LEN), lambda i: (0, i, 0, 0)),
        scratch_shapes=[pltpu.VMEM((SUB * ROWS, LANES), jnp.float32)],
        compiler_params=pltpu.CompilerParams(vmem_limit_bytes=32 * 1024 * 1024),
        name="lags",
    )(crossed, inv_hi, inv_lo)
    return lagged.reshape(CHAN_ROWS, LANES // 2, SEG_LEN)


def solution(mesh):
    n_chan, n_tm = mesh.shape["chan"], mesh.shape["tm"]
    return jax.shard_map(
        functools.partial(body, n_chan, n_tm),
        mesh=mesh,
        in_specs=(P("chan", "tm"), P("chan"), P("chan", "tm")),
        out_specs=P("chan", "tm", None),
        check_vma=False,
    )
```

```python
import functools

import jax
import jax.numpy as jnp
import numpy as np
from jax import lax
from jax.experimental import pallas as pl
from jax.experimental.pallas import tpu as pltpu
from jax.sharding import PartitionSpec as P

SEG_LEN = 256
BINS = 128
HALF_WIN = 64
SMOOTH = 4
ROWS = 2 * BINS
LANES = 128
SUB = 16
CHAN_ROWS = 32
SEGS = 64
PER_LANE = LANES // CHAN_ROWS
MESH = pl.DeviceIdType.MESH


def split_table(table):
    high = table.astype(jnp.bfloat16)
    low = (table - high.astype(np.float32)).astype(jnp.bfloat16)
    return high, low


def make_tables():
    row_bin = np.arange(ROWS) // 2
    row_imag = np.arange(ROWS) % 2 == 1
    time = np.arange(SEG_LEN)
    phase = 2.0 * np.pi / SEG_LEN * (row_bin[:, None] * time[None, :] % SEG_LEN)
    forward = np.where(row_imag[:, None], -np.sin(phase), np.cos(phase)).astype(np.float32)
    lag = np.arange(SEG_LEN) - BINS
    back = 2.0 * np.pi / SEG_LEN * (row_bin[:, None] * lag[None, :] % SEG_LEN)
    inverse = np.where(row_imag[:, None], -np.sin(back), np.cos(back))
    inverse = (inverse * (row_bin > 0)[:, None]).astype(np.float32)
    smooth = np.abs(row_bin[:, None] - row_bin[None, :]) <= SMOOTH
    sample_in = np.arange(2 * SEG_LEN)[:, None] - SEG_LEN // 2
    sample_out = np.arange(SEG_LEN)[None, :]
    box = np.abs(sample_in - sample_out) <= HALF_WIN
    return (
        split_table(forward),
        split_table(inverse),
        smooth.astype(jnp.bfloat16),
        box.astype(jnp.bfloat16),
    )


def halves(value):
    high = value.astype(jnp.bfloat16)
    return high, (value - high.astype(jnp.float32)).astype(jnp.bfloat16)


def mm(a, b, dims=((1,), (0,))):
    return lax.dot_general(a, b, (dims, ((), ())), preferred_element_type=jnp.float32)


NT = ((1,), (1,))
TN = ((0,), (0,))


def spread_kernel(
    n_chan, n_tm, piece,
    x_hbm, table_hbm, live_ref, valid_ref,
    out_hbm,
    xpad, tables, mask_rows, turned, send1, recv1, pair, cross, send2,
    halo_send, halo_recv, local_sem, send1_sem, recv1_sem, send2_sem, recv2_sem,
):
    n = n_chan * n_tm
    span = SEGS * SEG_LEN
    bins = BINS // n
    pieces = bins // piece
    chan, tm = lax.axis_index("chan"), lax.axis_index("tm")
    me = chan * n_tm + tm

    def device(index):
        return {"chan": index // n_tm, "tm": lax.rem(index, n_tm)}

    load = pltpu.make_async_copy(table_hbm, tables, local_sem.at[1])
    load.start()
    fill = pltpu.make_async_copy(x_hbm, xpad.at[:, pl.ds(LANES, span)], local_sem.at[0])
    fill.start()

    barrier = pltpu.get_barrier_semaphore()

    def greet(k, _):
        pl.semaphore_signal(
            barrier, inc=1, device_id=device(lax.rem(me + k, n)), device_id_type=MESH
        )
        return 0

    lax.fori_loop(1, n, greet, 0)

    to_left = pltpu.make_async_remote_copy(
        src_ref=x_hbm.at[:, pl.ds(0, LANES)],
        dst_ref=xpad.at[:, pl.ds(LANES + span, LANES)],
        send_sem=halo_send.at[0], recv_sem=halo_recv.at[0],
        device_id={"chan": chan, "tm": jnp.maximum(tm - 1, 0)}, device_id_type=MESH,
    )
    to_right = pltpu.make_async_remote_copy(
        src_ref=x_hbm.at[:, pl.ds(span - LANES, LANES)],
        dst_ref=xpad.at[:, pl.ds(0, LANES)],
        send_sem=halo_send.at[1], recv_sem=halo_recv.at[1],
        device_id={"chan": chan, "tm": jnp.minimum(tm + 1, n_tm - 1)}, device_id_type=MESH,
    )
    has_left, has_right = tm > 0, tm < n_tm - 1

    @pl.when(jnp.logical_not(has_left))
    def _():
        xpad[:, 0:LANES] = jnp.zeros((CHAN_ROWS, LANES), jnp.float32)

    @pl.when(jnp.logical_not(has_right))
    def _():
        xpad[:, LANES + span : 2 * LANES + span] = jnp.zeros((CHAN_ROWS, LANES), jnp.float32)

    valid = valid_ref[...].astype(jnp.float32).astype(jnp.bfloat16)
    live = live_ref[...].astype(jnp.float32)
    mask_sum = jnp.zeros((SUB, LANES), jnp.float32)
    seg_row = lax.broadcasted_iota(jnp.int32, (SUB, SEGS), 0) * PER_LANE
    seg_col = lax.broadcasted_iota(jnp.int32, (SUB, SEGS), 1)
    chan_row = lax.broadcasted_iota(jnp.int32, (CHAN_ROWS, LANES), 0)
    chan_lane = lax.broadcasted_iota(jnp.int32, (CHAN_ROWS, LANES), 1)
    for q in range(PER_LANE):
        pick = (seg_col == seg_row + q).astype(jnp.float32).astype(jnp.bfloat16)
        place = (chan_lane == chan_row + q * CHAN_ROWS).astype(jnp.float32).astype(jnp.bfloat16)
        picked = (mm(pick, valid, NT) * live).astype(jnp.bfloat16)
        mask_sum = mask_sum + mm(picked, place)
    mask_rows[...] = mask_sum

    pl.semaphore_wait(barrier, n - 1)

    @pl.when(has_left)
    def _():
        to_left.start()

    @pl.when(has_right)
    def _():
        to_right.start()

    row = lax.broadcasted_iota(jnp.int32, (ROWS, 2 * LANES), 0)

    def whiten(m, slot):
        window = jnp.concatenate(
            [
                xpad[:, pl.ds(pl.multiple_of(m * 8 * SEG_LEN + i * SEG_LEN, LANES), 2 * SEG_LEN)]
                for i in range(8)
            ],
            axis=0,
        )
        box = tables[3 * ROWS : 5 * ROWS]
        high, low = halves(jnp.abs(window))
        level = (mm(high, box) + mm(low, box)) * (1.0 / (2 * HALF_WIN + 1))
        normed = window[:, SEG_LEN // 2 : SEG_LEN // 2 + SEG_LEN] / (level + 1e-5)
        high, low = halves(normed)
        fwd_hi = tables[0:ROWS]
        spectrum = mm(fwd_hi, high, NT) + mm(fwd_hi, low, NT) + mm(tables[ROWS : 2 * ROWS], high, NT)
        power = spectrum * spectrum
        high, low = halves(power)
        smooth = tables[2 * ROWS : 3 * ROWS]
        smoothed = (mm(smooth, high) + mm(smooth, low)) * (1.0 / (2 * SMOOTH + 1))
        mean_power = jnp.sum(power, axis=0, keepdims=True) * (1.0 / BINS)
        mask = jnp.concatenate(
            [mask_rows[pl.ds(2 * m, 1), :], mask_rows[pl.ds(2 * m + 1, 1), :]], axis=1
        )
        whitened = spectrum * (mask * lax.rsqrt(smoothed + (0.1 * mean_power + 1e-6)))
        whitened = jnp.where(row == 0, mask, jnp.where(row == 1, 0.0, whitened))
        for u in range(2):
            turned[pl.ds(pl.multiple_of((2 * slot + u) * ROWS, ROWS), ROWS), :] = whitened[
                :, u * LANES : (u + 1) * LANES
            ]

    def exchange(source, target, size, place, send_sem, recv_sem, sems, local):
        def copy(part, spot, to, at):
            return pltpu.make_async_remote_copy(
                src_ref=source.at[pl.ds(place(part), size)],
                dst_ref=target.at[pl.ds(place(spot), size)],
                send_sem=send_sem.at[sems + to], recv_sem=recv_sem.at[sems + at],
                device_id=device(to), device_id_type=MESH,
            )

        own = pltpu.make_async_copy(
            source.at[pl.ds(place(me), size)], target.at[pl.ds(place(me), size)], local
        )

        def start():
            def one(k, _):
                to = lax.rem(me + k, n)
                copy(to, me, to, me).start()
                return 0

            lax.fori_loop(1, n, one, 0)
            own.start()

        def arrive(frm):
            copy(frm, frm, frm, frm).wait_recv()

        def leave():
            def one(k, _):
                to = lax.rem(me + k, n)
                copy(to, me, to, me).wait_send()
                return 0

            lax.fori_loop(1, n, one, 0)

        return start, own.wait, arrive, leave

    def spread(h):
        return exchange(
            send1, recv1, bins, lambda d: h * BINS + d * bins,
            send1_sem, recv1_sem, h * n, local_sem.at[2 + h],
        )

    fill.wait()
    load.wait()

    def half(h, _):
        def two(p, _):
            @pl.when(jnp.logical_and(h + p == 1, jnp.logical_and(p == 1, has_left)))
            def _():
                to_left.wait_send()
                to_right.wait_recv()

            @pl.when(jnp.logical_and(h + p == 2, has_right))
            def _():
                to_right.wait_send()
                to_left.wait_recv()

            first = jnp.where(h == 0, 1 + 2 * p, 4 + 2 * p)
            second = jnp.where(h == 0, 2 - 2 * p, 5 + 2 * p)
            whiten(first, first - 4 * h)
            whiten(second, second - 4 * h)
            return 0

        lax.fori_loop(0, 2, two, 0)

        def turn(step, _):
            for i in range(8):
                f = step * 8 + i
                tile = jnp.concatenate(
                    [turned[pl.ds(2 * f + c, SUB // 2, stride=ROWS), :] for c in range(2)], axis=0
                )
                send1[h * BINS + f] = tile.astype(jnp.bfloat16)
            return 0

        lax.fori_loop(0, BINS // 8, turn, 0)
        spread(h)[0]()
        return 0

    lax.fori_loop(0, 2, half, 0)

    lane = lax.broadcasted_iota(jnp.int32, (SUB, LANES), 1)
    low_half = lane < LANES // 2
    even = lax.rem(lane // CHAN_ROWS, 2) == 0
    n_all = n_chan * CHAN_ROWS
    depth = 2 * n_tm * SEGS
    groups = n_chan // PER_LANE

    def swap(first, second, distance, keep):
        return (
            jnp.where(keep, first, pltpu.roll(second, distance, 1)),
            jnp.where(keep, pltpu.roll(first, LANES - distance, 1), second),
        )

    def gather(h, _):
        _, own_wait, arrive, _ = spread(h)
        own_wait()

        def group(j, _):
            b = lax.rem(j, n_tm)
            g = lax.rem(chan // PER_LANE + j // n_tm, groups)
            sources = [(g * PER_LANE + i) * n_tm + b for i in range(PER_LANE)]
            for source in sources:
                @pl.when(source != me)
                def _():
                    arrive(source)

            for f in range(bins):
                tiles = [
                    recv1[h * BINS + source * bins + f].astype(jnp.float32) for source in sources
                ]
                p0, p2 = swap(tiles[0], tiles[2], 64, low_half)
                p1, p3 = swap(tiles[1], tiles[3], 64, low_half)
                u0, u1 = swap(p0, p1, 32, even)
                u2, u3 = swap(p2, p3, 32, even)
                for q, value in enumerate((u0, u1, u2, u3)):
                    at = pl.multiple_of(
                        f * depth + ((h * n_tm + b) * PER_LANE + q) * SUB, SUB
                    )
                    left = pl.multiple_of(g * LANES, LANES)
                    right = pl.multiple_of(n_all + g * LANES, LANES)
                    other = jnp.concatenate([value[SUB // 2 :], -value[: SUB // 2]], axis=0)
                    pair[pl.ds(at, SUB), pl.ds(left, LANES)] = value.astype(jnp.bfloat16)
                    pair[pl.ds(at, SUB), pl.ds(right, LANES)] = other.astype(jnp.bfloat16)
            return 0

        lax.fori_loop(0, n // PER_LANE, group, 0)
        return 0

    lax.fori_loop(0, 2, gather, 0)

    def back(s):
        return exchange(
            send2, out_hbm, 2 * piece, lambda d: (d * bins + s * piece) * 2,
            send2_sem, recv2_sem, s * n, local_sem.at[4 + s],
        )

    def some_bins(s, _):
        for i in range(piece):
            at = pl.multiple_of((s * piece + i) * depth, depth)
            cross[i] = mm(pair[pl.ds(at, depth), :n_all], pair[pl.ds(at, depth), :], TN)
        for i in range(piece):
            f = s * piece + i
            counts = jnp.logical_and(me == 0, f == 0)
            for a in range(n_chan):
                for p in range(n_tm // 2):
                    tops = []
                    for c in range(2):
                        at = c * n_all + p * LANES
                        top = cross[i, a * CHAN_ROWS : a * CHAN_ROWS + SUB, at : at + LANES]
                        bottom = cross[
                            i, a * CHAN_ROWS + SUB : (a + 1) * CHAN_ROWS, at : at + LANES
                        ]
                        tops.append(swap(top, bottom, 64, low_half))
                    for e in range(2):
                        dest = ((a * n_tm + 2 * p + e) * bins + f) * 2
                        real = tops[0][e].astype(jnp.bfloat16)
                        imag = tops[1][e]
                        if i == 0:
                            rest = tops[0][e] - real.astype(jnp.float32)
                            imag = jnp.where(counts, rest, imag)
                        send2[dest] = real
                        send2[dest + 1] = imag.astype(jnp.bfloat16)
        back(s)[0]()
        return 0

    lax.fori_loop(0, pieces, some_bins, 0)

    def finish(s, _):
        _, own_wait, arrive, leave = back(s)
        own_wait()

        def one(k, _):
            arrive(lax.rem(me + n - k, n))
            return 0

        lax.fori_loop(1, n, one, 0)
        leave()
        return 0

    lax.fori_loop(0, pieces, finish, 0)

    def done(h, _):
        spread(h)[3]()
        return 0

    lax.fori_loop(0, 2, done, 0)


def lag_kernel(steps, cross_ref, inverse_ref, out_ref, rows, scale):
    step = pl.program_id(0)

    @pl.when(step == 0)
    def _():
        count = cross_ref[0].astype(jnp.float32) + cross_ref[1].astype(jnp.float32)
        scale[...] = (2.0 / jnp.maximum(count, 1.0)).T

        def turn(block, _):
            for i in range(16):
                r = block * 16 + i
                rows[pl.ds(r, SUB, stride=ROWS), :] = cross_ref[r].astype(jnp.float32)
            return 0

        lax.fori_loop(0, ROWS // 16, turn, 0)

    column = lax.broadcasted_iota(jnp.int32, (LANES, SUB), 1)
    for i in range(SUB // steps):
        index = step * (SUB // steps) + i
        value = rows[pl.ds(pl.multiple_of(index * ROWS, ROWS), ROWS), :].astype(jnp.bfloat16)
        lagged = mm(value, inverse_ref[:ROWS], TN) + mm(value, inverse_ref[ROWS:], TN)
        lagged = lagged * jnp.sum(
            jnp.where(column == index, scale[...], 0.0), axis=1, keepdims=True
        )
        out_ref[0, i] = lagged[: LANES // 2]
        out_ref[1, i] = lagged[LANES // 2 :]


def body(n_chan, n_tm, traces, live_channel, valid_segment):
    forward, inverse, smooth, box = make_tables()
    n = n_chan * n_tm
    n_all = n_chan * CHAN_ROWS
    bins = BINS // n
    piece = min(2, bins)
    pieces = bins // piece
    span = traces.shape[1]
    tables = np.concatenate([*forward, smooth, box], axis=0)
    inverse = np.concatenate(inverse, axis=0)
    vmem = pl.BlockSpec(memory_space=pltpu.VMEM)
    hbm = pl.BlockSpec(memory_space=pltpu.HBM)
    dma = pltpu.SemaphoreType.DMA
    tiles = (ROWS, SUB, LANES)
    crossed = pl.pallas_call(
        functools.partial(spread_kernel, n_chan, n_tm, piece),
        out_shape=jax.ShapeDtypeStruct(tiles, jnp.bfloat16),
        in_specs=[hbm, hbm, vmem, vmem],
        out_specs=hbm,
        scratch_shapes=[
            pltpu.VMEM((CHAN_ROWS, span + 2 * LANES), jnp.float32),
            pltpu.VMEM(tables.shape, jnp.bfloat16),
            pltpu.VMEM((SUB, LANES), jnp.float32),
            pltpu.VMEM((SUB // 2 * ROWS, LANES), jnp.float32),
            pltpu.VMEM(tiles, jnp.bfloat16),
            pltpu.VMEM(tiles, jnp.bfloat16),
            pltpu.VMEM((bins * 2 * n_tm * SEGS, 2 * n_all), jnp.bfloat16),
            pltpu.VMEM((piece, n_all, 2 * n_all), jnp.float32),
            pltpu.VMEM(tiles, jnp.bfloat16),
            dma((2,)), dma((2,)), dma((4 + pieces,)),
            dma((2 * n,)), dma((2 * n,)), dma((pieces * n,)), dma((pieces * n,)),
        ],
        compiler_params=pltpu.CompilerParams(
            collective_id=0, has_side_effects=True, vmem_limit_bytes=40 * 1024 * 1024
        ),
        name="spread",
    )(traces, tables, live_channel.reshape(1, CHAN_ROWS), valid_segment)
    steps = 4
    lagged = pl.pallas_call(
        functools.partial(lag_kernel, steps),
        out_shape=jax.ShapeDtypeStruct((2, SUB, LANES // 2, SEG_LEN), jnp.float32),
        grid=(steps,),
        in_specs=[
            pl.BlockSpec(tiles, lambda i: (0, 0, 0)),
            pl.BlockSpec((2 * ROWS, SEG_LEN), lambda i: (0, 0)),
        ],
        out_specs=pl.BlockSpec((2, SUB // steps, LANES // 2, SEG_LEN), lambda i: (0, i, 0, 0)),
        scratch_shapes=[
            pltpu.VMEM((SUB * ROWS, LANES), jnp.float32),
            pltpu.VMEM((LANES, SUB), jnp.float32),
        ],
        compiler_params=pltpu.CompilerParams(vmem_limit_bytes=32 * 1024 * 1024),
        name="lags",
    )(crossed, inverse)
    return lagged.reshape(CHAN_ROWS, LANES // 2, SEG_LEN)


def solution(mesh):
    n_chan, n_tm = mesh.shape["chan"], mesh.shape["tm"]
    return jax.shard_map(
        functools.partial(body, n_chan, n_tm),
        mesh=mesh,
        in_specs=(P("chan", "tm"), P("chan"), P("chan", "tm")),
        out_specs=P("chan", "tm", None),
        check_vma=False,
    )
```

```python
import functools

import jax
import jax.numpy as jnp
import numpy as np
from jax import lax
from jax.experimental import pallas as pl
from jax.experimental.pallas import tpu as pltpu
from jax.sharding import PartitionSpec as P

SEG_LEN = 256
BINS = 128
HALF_WIN = 64
SMOOTH = 4
ROWS = 2 * BINS
LANES = 128
SUB = 16
CHAN_ROWS = 32
SEGS = 64
PER_LANE = LANES // CHAN_ROWS
MESH = pl.DeviceIdType.MESH
VMEM_LIMIT = 63 * 1024 * 1024


def split_table(table):
    high = table.astype(jnp.bfloat16)
    low = (table - high.astype(np.float32)).astype(jnp.bfloat16)
    return high, low


def make_tables():
    row_bin = np.arange(ROWS) // 2
    row_imag = np.arange(ROWS) % 2 == 1
    time = np.arange(SEG_LEN)
    phase = 2.0 * np.pi / SEG_LEN * (row_bin[:, None] * time[None, :] % SEG_LEN)
    forward = np.where(row_imag[:, None], -np.sin(phase), np.cos(phase)).astype(np.float32)
    lag = np.arange(SEG_LEN) - BINS
    back = 2.0 * np.pi / SEG_LEN * (row_bin[:, None] * lag[None, :] % SEG_LEN)
    inverse = np.where(row_imag[:, None], -np.sin(back), np.cos(back))
    inverse = (inverse * (row_bin > 0)[:, None]).astype(np.float32)
    smooth = np.abs(row_bin[:, None] - row_bin[None, :]) <= SMOOTH
    sample_in = np.arange(2 * SEG_LEN)[:, None] - SEG_LEN // 2
    sample_out = np.arange(SEG_LEN)[None, :]
    box = np.abs(sample_in - sample_out) <= HALF_WIN
    return (
        split_table(forward),
        split_table(inverse),
        smooth.astype(jnp.bfloat16),
        box.astype(jnp.bfloat16),
    )


def halves(value):
    high = value.astype(jnp.bfloat16)
    return high, (value - high.astype(jnp.float32)).astype(jnp.bfloat16)


def mm(a, b, dims=((1,), (0,))):
    return lax.dot_general(a, b, (dims, ((), ())), preferred_element_type=jnp.float32)


NT = ((1,), (1,))
TN = ((0,), (0,))


def spread_kernel(
    n_chan, n_tm, piece,
    x_hbm, table_hbm, live_ref, valid_ref,
    out_hbm,
    xpad, tables, mask_rows, turned, send1, recv1, near1, pair, near_pair, cross, near_cross, send2,
    halo_send, halo_recv, local_sem, send1_sem, recv1_sem, near_send, near_recv, send2_sem, recv2_sem,
):
    n = n_chan * n_tm
    span = SEGS * SEG_LEN
    bins = BINS // n
    pieces = bins // piece
    chan, tm = lax.axis_index("chan"), lax.axis_index("tm")
    me = chan * n_tm + tm
    side = chan // (n_chan // 2)
    base = side * (n // 2)
    partner = lax.rem(me + n // 2, n)

    def device(index):
        return {"chan": index // n_tm, "tm": lax.rem(index, n_tm)}

    load = pltpu.make_async_copy(table_hbm, tables, local_sem.at[1])
    load.start()
    fill = pltpu.make_async_copy(x_hbm, xpad.at[:, pl.ds(LANES, span)], local_sem.at[0])
    fill.start()

    barrier = pltpu.get_barrier_semaphore()

    def greet(k, _):
        pl.semaphore_signal(
            barrier, inc=1, device_id=device(lax.rem(me + k, n)), device_id_type=MESH
        )
        return 0

    lax.fori_loop(1, n, greet, 0)

    to_left = pltpu.make_async_remote_copy(
        src_ref=x_hbm.at[:, pl.ds(0, LANES)],
        dst_ref=xpad.at[:, pl.ds(LANES + span, LANES)],
        send_sem=halo_send.at[0], recv_sem=halo_recv.at[0],
        device_id={"chan": chan, "tm": jnp.maximum(tm - 1, 0)}, device_id_type=MESH,
    )
    to_right = pltpu.make_async_remote_copy(
        src_ref=x_hbm.at[:, pl.ds(span - LANES, LANES)],
        dst_ref=xpad.at[:, pl.ds(0, LANES)],
        send_sem=halo_send.at[1], recv_sem=halo_recv.at[1],
        device_id={"chan": chan, "tm": jnp.minimum(tm + 1, n_tm - 1)}, device_id_type=MESH,
    )
    has_left, has_right = tm > 0, tm < n_tm - 1

    @pl.when(jnp.logical_not(has_left))
    def _():
        xpad[:, 0:LANES] = jnp.zeros((CHAN_ROWS, LANES), jnp.float32)

    @pl.when(jnp.logical_not(has_right))
    def _():
        xpad[:, LANES + span : 2 * LANES + span] = jnp.zeros((CHAN_ROWS, LANES), jnp.float32)

    valid = valid_ref[...].astype(jnp.float32).astype(jnp.bfloat16)
    live = live_ref[...].astype(jnp.float32)
    mask_sum = jnp.zeros((SUB, LANES), jnp.float32)
    seg_row = lax.broadcasted_iota(jnp.int32, (SUB, SEGS), 0) * PER_LANE
    seg_col = lax.broadcasted_iota(jnp.int32, (SUB, SEGS), 1)
    chan_row = lax.broadcasted_iota(jnp.int32, (CHAN_ROWS, LANES), 0)
    chan_lane = lax.broadcasted_iota(jnp.int32, (CHAN_ROWS, LANES), 1)
    for q in range(PER_LANE):
        pick = (seg_col == seg_row + q).astype(jnp.float32).astype(jnp.bfloat16)
        place = (chan_lane == chan_row + q * CHAN_ROWS).astype(jnp.float32).astype(jnp.bfloat16)
        picked = (mm(pick, valid, NT) * live).astype(jnp.bfloat16)
        mask_sum = mask_sum + mm(picked, place)
    mask_rows[...] = mask_sum

    pl.semaphore_wait(barrier, n - 1)

    @pl.when(has_left)
    def _():
        to_left.start()

    @pl.when(has_right)
    def _():
        to_right.start()

    row = lax.broadcasted_iota(jnp.int32, (ROWS, 2 * LANES), 0)

    def whiten(m, slot):
        window = jnp.concatenate(
            [
                xpad[:, pl.ds(pl.multiple_of(m * 8 * SEG_LEN + i * SEG_LEN, LANES), 2 * SEG_LEN)]
                for i in range(8)
            ],
            axis=0,
        )
        box = tables[3 * ROWS : 5 * ROWS]
        high, low = halves(jnp.abs(window))
        level = (mm(high, box) + mm(low, box)) * (1.0 / (2 * HALF_WIN + 1))
        normed = window[:, SEG_LEN // 2 : SEG_LEN // 2 + SEG_LEN] / (level + 1e-5)
        high, low = halves(normed)
        fwd_hi = tables[0:ROWS]
        spectrum = mm(fwd_hi, high, NT) + mm(fwd_hi, low, NT) + mm(tables[ROWS : 2 * ROWS], high, NT)
        power = spectrum * spectrum
        high, low = halves(power)
        smooth = tables[2 * ROWS : 3 * ROWS]
        smoothed = (mm(smooth, high) + mm(smooth, low)) * (1.0 / (2 * SMOOTH + 1))
        mean_power = jnp.sum(power, axis=0, keepdims=True) * (1.0 / BINS)
        mask = jnp.concatenate(
            [mask_rows[pl.ds(2 * m, 1), :], mask_rows[pl.ds(2 * m + 1, 1), :]], axis=1
        )
        whitened = spectrum * (mask * lax.rsqrt(smoothed + (0.1 * mean_power + 1e-6)))
        whitened = jnp.where(row == 0, mask, jnp.where(row == 1, 0.0, whitened))
        for u in range(2):
            turned[pl.ds(pl.multiple_of((2 * slot + u) * ROWS, ROWS), ROWS), :] = whitened[
                :, u * LANES : (u + 1) * LANES
            ]

    def send(source, target, size, place_out, place_in, out_sem, in_sem, to):
        return pltpu.make_async_remote_copy(
            src_ref=source.at[pl.ds(place_out, size)], dst_ref=target.at[pl.ds(place_in, size)],
            send_sem=out_sem, recv_sem=in_sem, device_id=device(to), device_id_type=MESH,
        )

    def far(h, to, owner):
        return send(
            send1, recv1, bins, h * BINS + to * bins, h * BINS + owner * bins,
            send1_sem.at[h * n + to], recv1_sem.at[h * n + owner], to,
        )

    def near(h, to, owner):
        return send(
            send1, near1, bins, h * BINS + lax.rem(base + to + n // 2, n) * bins,
            (h * (n // 2) + owner) * bins,
            near_send.at[h * (n // 2) + to], near_recv.at[h * (n // 2) + owner], base + to,
        )

    def keep_far(h):
        return pltpu.make_async_copy(
            send1.at[pl.ds(h * BINS + me * bins, bins)],
            recv1.at[pl.ds(h * BINS + me * bins, bins)], local_sem.at[2 + h],
        )

    def keep_near(h):
        return pltpu.make_async_copy(
            send1.at[pl.ds(h * BINS + partner * bins, bins)],
            near1.at[pl.ds((h * (n // 2) + me - base) * bins, bins)], local_sem.at[4 + h],
        )

    def each_far(act):
        def one(k, _):
            act(lax.rem(me + k, n))
            return 0

        lax.fori_loop(1, n, one, 0)

    def each_near(act):
        def one(k, _):
            act(lax.rem(me - base + k, n // 2))
            return 0

        lax.fori_loop(1, n // 2, one, 0)

    fill.wait()
    load.wait()

    def half(h, _):
        def two(p, _):
            @pl.when(jnp.logical_and(h + p == 1, jnp.logical_and(p == 1, has_left)))
            def _():
                to_left.wait_send()
                to_right.wait_recv()

            @pl.when(jnp.logical_and(h + p == 2, has_right))
            def _():
                to_right.wait_send()
                to_left.wait_recv()

            first = jnp.where(h == 0, 1 + 2 * p, 4 + 2 * p)
            second = jnp.where(h == 0, 2 - 2 * p, 5 + 2 * p)
            whiten(first, first - 4 * h)
            whiten(second, second - 4 * h)
            return 0

        lax.fori_loop(0, 2, two, 0)

        def turn(step, _):
            for i in range(8):
                f = step * 8 + i
                tile = jnp.concatenate(
                    [turned[pl.ds(2 * f + c, SUB // 2, stride=ROWS), :] for c in range(2)], axis=0
                )
                send1[h * BINS + f] = tile.astype(jnp.bfloat16)
            return 0

        lax.fori_loop(0, BINS // 8, turn, 0)
        each_far(lambda to: far(h, to, me).start())
        each_near(lambda to: near(h, to, me - base).start())
        keep_far(h).start()
        keep_near(h).start()
        return 0

    lax.fori_loop(0, 2, half, 0)

    lane = lax.broadcasted_iota(jnp.int32, (SUB, LANES), 1)
    low_half = lane < LANES // 2
    even = lax.rem(lane // CHAN_ROWS, 2) == 0
    n_all = n_chan * CHAN_ROWS
    depth = 2 * n_tm * SEGS
    groups = n_chan // PER_LANE

    def swap(first, second, distance, keep):
        return (
            jnp.where(keep, first, pltpu.roll(second, distance, 1)),
            jnp.where(keep, pltpu.roll(first, LANES - distance, 1), second),
        )

    def arrange(tiles, into, width, at, g):
        p0, p2 = swap(tiles[0], tiles[2], 64, low_half)
        p1, p3 = swap(tiles[1], tiles[3], 64, low_half)
        u0, u1 = swap(p0, p1, 32, even)
        u2, u3 = swap(p2, p3, 32, even)
        left = pl.multiple_of(g * LANES, LANES)
        right = pl.multiple_of(width + g * LANES, LANES)
        for q, value in enumerate((u0, u1, u2, u3)):
            rows = pl.ds(pl.multiple_of(at + q * SUB, SUB), SUB)
            other = jnp.concatenate([value[SUB // 2 :], -value[: SUB // 2]], axis=0)
            into[rows, pl.ds(left, LANES)] = value.astype(jnp.bfloat16)
            into[rows, pl.ds(right, LANES)] = other.astype(jnp.bfloat16)

    def gather(h, _):
        keep_far(h).wait()
        keep_near(h).wait()

        def near_group(j, _):
            b = lax.rem(j, n_tm)
            g = j // n_tm
            sources = [(g * PER_LANE + i) * n_tm + b for i in range(PER_LANE)]
            for source in sources:
                @pl.when(source != me - base)
                def _():
                    near(h, source, source).wait_recv()

            for f in range(bins):
                tiles = [
                    near1[(h * (n // 2) + source) * bins + f].astype(jnp.float32)
                    for source in sources
                ]
                arrange(tiles, near_pair, n_half, f * depth + (h * n_tm + b) * PER_LANE * SUB, g)
            return 0

        lax.fori_loop(0, n // 2 // PER_LANE, near_group, 0)

        def far_group(j, _):
            b = lax.rem(j, n_tm)
            g = lax.rem(chan // PER_LANE + j // n_tm, groups)
            sources = [(g * PER_LANE + i) * n_tm + b for i in range(PER_LANE)]
            for source in sources:
                @pl.when(source != me)
                def _():
                    far(h, source, source).wait_recv()

            for f in range(bins):
                tiles = [
                    recv1[h * BINS + source * bins + f].astype(jnp.float32) for source in sources
                ]
                arrange(tiles, pair, n_all, f * depth + (h * n_tm + b) * PER_LANE * SUB, g)
            return 0

        lax.fori_loop(0, n // PER_LANE, far_group, 0)
        return 0

    n_half = n_all // 2
    lax.fori_loop(0, 2, gather, 0)

    half_a, half_b = n_chan // 2, n_tm // 2
    paired = tm // half_b == side

    def back(s, slot, mine):
        a, b = slot // n_tm, lax.rem(slot, n_tm)
        spare = jnp.logical_and(a // half_a != side, b // half_b != side)
        moved = lax.rem(a + half_a, n_chan) * n_tm + lax.rem(b + half_b, n_tm)
        to = jnp.where(spare, moved, slot)
        owner = jnp.where(spare, partner, me) if mine else slot
        return to, send(
            send2, out_hbm, 2 * piece, (slot * bins + s * piece) * 2,
            (owner * bins + s * piece) * 2,
            send2_sem.at[s * n + slot], recv2_sem.at[s * n + owner], to,
        )

    def keep_back(s):
        return pltpu.make_async_copy(
            send2.at[pl.ds((me * bins + s * piece) * 2, 2 * piece)],
            out_hbm.at[pl.ds((me * bins + s * piece) * 2, 2 * piece)], local_sem.at[6 + 2 * s],
        )

    def keep_spare(s):
        slot = lax.rem(chan + half_a, n_chan) * n_tm + lax.rem(tm + half_b, n_tm)
        return pltpu.make_async_copy(
            send2.at[pl.ds((slot * bins + s * piece) * 2, 2 * piece)],
            out_hbm.at[pl.ds((partner * bins + s * piece) * 2, 2 * piece)],
            local_sem.at[7 + 2 * s],
        )

    def some_bins(s, _):
        for i in range(piece):
            at = pl.ds(pl.multiple_of((s * piece + i) * depth, depth), depth)
            cross[i] = mm(pair[at, :n_all], pair[at, :], TN)
            near_cross[i] = mm(near_pair[at, :n_half], near_pair[at, :], TN)

        def pack(block, width, i, row, lane_block, owner, slot_a, slot_b):
            f = s * piece + i
            at = pl.multiple_of(row * CHAN_ROWS, CHAN_ROWS)
            tops = []
            for c in range(2):
                lanes = pl.ds(pl.multiple_of(c * width + lane_block * LANES, LANES), LANES)
                top = block[i, pl.ds(at, SUB), lanes]
                bottom = block[i, pl.ds(at + SUB, SUB), lanes]
                tops.append(swap(top, bottom, 64, low_half))
            for e in range(2):
                dest = ((slot_a * n_tm + slot_b + e) * bins + f) * 2
                real = tops[0][e].astype(jnp.bfloat16)
                imag = tops[1][e]
                if i == 0:
                    rest = tops[0][e] - real.astype(jnp.float32)
                    imag = jnp.where(jnp.logical_and(owner == 0, f == 0), rest, imag)
                send2[dest] = real
                send2[dest + 1] = imag.astype(jnp.bfloat16)

        for i in range(piece):
            for k in range(half_a):
                mine, others = side * half_a + k, (1 - side) * half_a + k
                for p in range(n_tm // 2):
                    pack(cross, n_all, i, mine, p, me, mine, 2 * p)
                for p in range(half_b // 2):
                    inside = side * (half_b // 2) + p
                    pack(cross, n_all, i, others, inside, me, others, 2 * inside)
                    pack(
                        near_cross, n_half, i, k, p, partner, others,
                        (1 - side) * half_b + 2 * p,
                    )

        def one(k, _):
            to, copy = back(s, lax.rem(me + k, n), True)

            @pl.when(to != me)
            def _():
                copy.start()

            return 0

        lax.fori_loop(1, n, one, 0)
        keep_back(s).start()

        @pl.when(paired)
        def _():
            keep_spare(s).start()

        return 0

    lax.fori_loop(0, pieces, some_bins, 0)

    def finish(s, _):
        keep_back(s).wait()

        @pl.when(paired)
        def _():
            keep_spare(s).wait()

        def one(k, _):
            owner = lax.rem(me + n - k, n)

            @pl.when(jnp.logical_not(jnp.logical_and(paired, owner == partner)))
            def _():
                back(s, owner, False)[1].wait_recv()

            to, copy = back(s, lax.rem(me + k, n), True)

            @pl.when(to != me)
            def _():
                copy.wait_send()

            return 0

        lax.fori_loop(1, n, one, 0)
        return 0

    lax.fori_loop(0, pieces, finish, 0)

    def done(h, _):
        each_far(lambda to: far(h, to, me).wait_send())
        each_near(lambda to: near(h, to, me - base).wait_send())
        return 0

    lax.fori_loop(0, 2, done, 0)


def lag_kernel(steps, cross_ref, inverse_ref, out_ref, rows, scale):
    step = pl.program_id(0)

    @pl.when(step == 0)
    def _():
        count = cross_ref[0].astype(jnp.float32) + cross_ref[1].astype(jnp.float32)
        scale[...] = (2.0 / jnp.maximum(count, 1.0)).T

        def turn(block, _):
            for i in range(16):
                r = block * 16 + i
                rows[pl.ds(r, SUB, stride=ROWS), :] = cross_ref[r].astype(jnp.float32)
            return 0

        lax.fori_loop(0, ROWS // 16, turn, 0)

    column = lax.broadcasted_iota(jnp.int32, (LANES, SUB), 1)
    for i in range(SUB // steps):
        index = step * (SUB // steps) + i
        value = rows[pl.ds(pl.multiple_of(index * ROWS, ROWS), ROWS), :].astype(jnp.bfloat16)
        lagged = mm(value, inverse_ref[:ROWS], TN) + mm(value, inverse_ref[ROWS:], TN)
        lagged = lagged * jnp.sum(
            jnp.where(column == index, scale[...], 0.0), axis=1, keepdims=True
        )
        out_ref[0, i] = lagged[: LANES // 2]
        out_ref[1, i] = lagged[LANES // 2 :]


def body(n_chan, n_tm, traces, live_channel, valid_segment):
    forward, inverse, smooth, box = make_tables()
    n = n_chan * n_tm
    n_all = n_chan * CHAN_ROWS
    bins = BINS // n
    piece = min(2, bins)
    pieces = bins // piece
    span = traces.shape[1]
    tables = np.concatenate([*forward, smooth, box], axis=0)
    inverse = np.concatenate(inverse, axis=0)
    vmem = pl.BlockSpec(memory_space=pltpu.VMEM)
    hbm = pl.BlockSpec(memory_space=pltpu.HBM)
    dma = pltpu.SemaphoreType.DMA
    tiles = (ROWS, SUB, LANES)
    crossed = pl.pallas_call(
        functools.partial(spread_kernel, n_chan, n_tm, piece),
        out_shape=jax.ShapeDtypeStruct(tiles, jnp.bfloat16),
        in_specs=[hbm, hbm, vmem, vmem],
        out_specs=hbm,
        scratch_shapes=[
            pltpu.VMEM((CHAN_ROWS, span + 2 * LANES), jnp.float32),
            pltpu.VMEM(tables.shape, jnp.bfloat16),
            pltpu.VMEM((SUB, LANES), jnp.float32),
            pltpu.VMEM((SUB // 2 * ROWS, LANES), jnp.float32),
            pltpu.VMEM(tiles, jnp.bfloat16),
            pltpu.VMEM(tiles, jnp.bfloat16),
            pltpu.VMEM((BINS, SUB, LANES), jnp.bfloat16),
            pltpu.VMEM((bins * 2 * n_tm * SEGS, 2 * n_all), jnp.bfloat16),
            pltpu.VMEM((bins * 2 * n_tm * SEGS, n_all), jnp.bfloat16),
            pltpu.VMEM((piece, n_all, 2 * n_all), jnp.float32),
            pltpu.VMEM((piece, n_all // 2, n_all), jnp.float32),
            pltpu.VMEM(tiles, jnp.bfloat16),
            dma((2,)), dma((2,)), dma((6 + 2 * pieces,)),
            dma((2 * n,)), dma((2 * n,)), dma((n,)), dma((n,)),
            dma((pieces * n,)), dma((pieces * n,)),
        ],
        compiler_params=pltpu.CompilerParams(
            collective_id=0, has_side_effects=True, vmem_limit_bytes=VMEM_LIMIT
        ),
        name="spread",
    )(traces, tables, live_channel.reshape(1, CHAN_ROWS), valid_segment)
    steps = 4
    lagged = pl.pallas_call(
        functools.partial(lag_kernel, steps),
        out_shape=jax.ShapeDtypeStruct((2, SUB, LANES // 2, SEG_LEN), jnp.float32),
        grid=(steps,),
        in_specs=[
            pl.BlockSpec(tiles, lambda i: (0, 0, 0)),
            pl.BlockSpec((2 * ROWS, SEG_LEN), lambda i: (0, 0)),
        ],
        out_specs=pl.BlockSpec((2, SUB // steps, LANES // 2, SEG_LEN), lambda i: (0, i, 0, 0)),
        scratch_shapes=[
            pltpu.VMEM((SUB * ROWS, LANES), jnp.float32),
            pltpu.VMEM((LANES, SUB), jnp.float32),
        ],
        compiler_params=pltpu.CompilerParams(vmem_limit_bytes=VMEM_LIMIT),
        name="lags",
    )(crossed, inverse)
    return lagged.reshape(CHAN_ROWS, LANES // 2, SEG_LEN)


def solution(mesh):
    n_chan, n_tm = mesh.shape["chan"], mesh.shape["tm"]
    return jax.shard_map(
        functools.partial(body, n_chan, n_tm),
        mesh=mesh,
        in_specs=(P("chan", "tm"), P("chan"), P("chan", "tm")),
        out_specs=P("chan", "tm", None),
        check_vma=False,
    )
```

```python
import functools

import jax
import jax.numpy as jnp
import numpy as np
from jax import lax
from jax.experimental import pallas as pl
from jax.experimental.pallas import tpu as pltpu
from jax.sharding import PartitionSpec as P

SEG_LEN = 256
BINS = 128
HALF_WIN = 64
SMOOTH = 4
ROWS = 2 * BINS
LANES = 128
SUB = 16
CHAN_ROWS = 32
SEGS = 64
PER_LANE = LANES // CHAN_ROWS
MESH = pl.DeviceIdType.MESH
VMEM_LIMIT = 63 * 1024 * 1024


def split_table(table):
    high = table.astype(jnp.bfloat16)
    low = (table - high.astype(np.float32)).astype(jnp.bfloat16)
    return high, low


def make_tables():
    row_bin = np.arange(ROWS) // 2
    row_imag = np.arange(ROWS) % 2 == 1
    time = np.arange(SEG_LEN)
    phase = 2.0 * np.pi / SEG_LEN * (row_bin[:, None] * time[None, :] % SEG_LEN)
    forward = np.where(row_imag[:, None], -np.sin(phase), np.cos(phase)).astype(np.float32)
    lag = np.arange(SEG_LEN) - BINS
    back = 2.0 * np.pi / SEG_LEN * (row_bin[:, None] * lag[None, :] % SEG_LEN)
    inverse = np.where(row_imag[:, None], -np.sin(back), np.cos(back))
    inverse = (inverse * (row_bin > 0)[:, None]).astype(np.float32)
    smooth = np.abs(row_bin[:, None] - row_bin[None, :]) <= SMOOTH
    sample_in = np.arange(2 * SEG_LEN)[:, None] - SEG_LEN // 2
    sample_out = np.arange(SEG_LEN)[None, :]
    box = np.abs(sample_in - sample_out) <= HALF_WIN
    return (
        split_table(forward),
        split_table(inverse),
        smooth.astype(jnp.bfloat16),
        box.astype(jnp.bfloat16),
    )


def halves(value):
    high = value.astype(jnp.bfloat16)
    return high, (value - high.astype(jnp.float32)).astype(jnp.bfloat16)


def mm(a, b, dims=((1,), (0,))):
    return lax.dot_general(a, b, (dims, ((), ())), preferred_element_type=jnp.float32)


NT = ((1,), (1,))
TN = ((0,), (0,))


def spread_kernel(
    n_chan, n_tm, piece,
    x_hbm, table_hbm, live_hbm, valid_hbm,
    out_hbm,
    live_ref, valid_ref, xpad, tables, mask_rows, turned, send1, recv1, near1, pair, near_pair, cross, near_cross, send2,
    halo_send, halo_recv, local_sem, send1_sem, recv1_sem, near_send, near_recv, send2_sem, recv2_sem,
):
    n = n_chan * n_tm
    span = SEGS * SEG_LEN
    bins = BINS // n
    pieces = bins // piece
    chan, tm = lax.axis_index("chan"), lax.axis_index("tm")
    me = chan * n_tm + tm
    half_a, half_b = n_chan // 2, n_tm // 2

    def wrap(index, count):
        return jnp.where(index >= count, index - count, index)

    def upper(index, half):
        return (index >= half).astype(jnp.int32)

    side = upper(chan, half_a)
    near_chan = chan - side * half_a
    near_me = near_chan * n_tm + tm
    partner = wrap(chan + half_a, n_chan) * n_tm + tm

    def device(a, b):
        return {"chan": a, "tm": b}

    def others(first, count, act):
        for j in range(1, n_tm):
            act(first, wrap(tm + j, n_tm))

        def one(i, _):
            for j in range(n_tm):
                act(wrap(first + i, count), wrap(tm + j, n_tm))
            return 0

        lax.fori_loop(1, count, one, 0)

    live_in = pltpu.make_async_copy(live_hbm, live_ref, local_sem.at[6])
    live_in.start()
    valid_in = pltpu.make_async_copy(valid_hbm, valid_ref, local_sem.at[7])
    valid_in.start()
    load = pltpu.make_async_copy(table_hbm, tables, local_sem.at[1])
    load.start()
    fill = pltpu.make_async_copy(x_hbm, xpad.at[:, pl.ds(LANES, span)], local_sem.at[0])
    fill.start()

    barrier = pltpu.get_barrier_semaphore()

    others(
        chan, n_chan,
        lambda a, b: pl.semaphore_signal(
            barrier, inc=1, device_id=device(a, b), device_id_type=MESH
        ),
    )

    to_left = pltpu.make_async_remote_copy(
        src_ref=x_hbm.at[:, pl.ds(0, LANES)],
        dst_ref=xpad.at[:, pl.ds(LANES + span, LANES)],
        send_sem=halo_send.at[0], recv_sem=halo_recv.at[0],
        device_id={"chan": chan, "tm": jnp.maximum(tm - 1, 0)}, device_id_type=MESH,
    )
    to_right = pltpu.make_async_remote_copy(
        src_ref=x_hbm.at[:, pl.ds(span - LANES, LANES)],
        dst_ref=xpad.at[:, pl.ds(0, LANES)],
        send_sem=halo_send.at[1], recv_sem=halo_recv.at[1],
        device_id={"chan": chan, "tm": jnp.minimum(tm + 1, n_tm - 1)}, device_id_type=MESH,
    )
    has_left, has_right = tm > 0, tm < n_tm - 1

    @pl.when(jnp.logical_not(has_left))
    def _():
        xpad[:, 0:LANES] = jnp.zeros((CHAN_ROWS, LANES), jnp.float32)

    @pl.when(jnp.logical_not(has_right))
    def _():
        xpad[:, LANES + span : 2 * LANES + span] = jnp.zeros((CHAN_ROWS, LANES), jnp.float32)

    live_in.wait()
    valid_in.wait()
    valid = valid_ref[...].astype(jnp.float32).astype(jnp.bfloat16)
    live = live_ref[...].astype(jnp.float32)
    mask_sum = jnp.zeros((SUB, LANES), jnp.float32)
    seg_row = lax.broadcasted_iota(jnp.int32, (SUB, SEGS), 0) * PER_LANE
    seg_col = lax.broadcasted_iota(jnp.int32, (SUB, SEGS), 1)
    chan_row = lax.broadcasted_iota(jnp.int32, (CHAN_ROWS, LANES), 0)
    chan_lane = lax.broadcasted_iota(jnp.int32, (CHAN_ROWS, LANES), 1)
    for q in range(PER_LANE):
        pick = (seg_col == seg_row + q).astype(jnp.float32).astype(jnp.bfloat16)
        place = (chan_lane == chan_row + q * CHAN_ROWS).astype(jnp.float32).astype(jnp.bfloat16)
        picked = (mm(pick, valid, NT) * live).astype(jnp.bfloat16)
        mask_sum = mask_sum + mm(picked, place)
    mask_rows[...] = mask_sum

    pl.semaphore_wait(barrier, n - 1)

    @pl.when(has_left)
    def _():
        to_left.start()

    @pl.when(has_right)
    def _():
        to_right.start()

    row = lax.broadcasted_iota(jnp.int32, (ROWS, 2 * LANES), 0)

    def whiten(m, slot):
        window = jnp.concatenate(
            [
                xpad[:, pl.ds(pl.multiple_of(m * 8 * SEG_LEN + i * SEG_LEN, LANES), 2 * SEG_LEN)]
                for i in range(8)
            ],
            axis=0,
        )
        box = tables[3 * ROWS : 5 * ROWS]
        high, low = halves(jnp.abs(window))
        level = (mm(high, box) + mm(low, box)) * (1.0 / (2 * HALF_WIN + 1))
        normed = window[:, SEG_LEN // 2 : SEG_LEN // 2 + SEG_LEN] / (level + 1e-5)
        high, low = halves(normed)
        fwd_hi = tables[0:ROWS]
        spectrum = mm(fwd_hi, high, NT) + mm(fwd_hi, low, NT) + mm(tables[ROWS : 2 * ROWS], high, NT)
        power = spectrum * spectrum
        high, low = halves(power)
        smooth = tables[2 * ROWS : 3 * ROWS]
        smoothed = (mm(smooth, high) + mm(smooth, low)) * (1.0 / (2 * SMOOTH + 1))
        mean_power = jnp.sum(power, axis=0, keepdims=True) * (1.0 / BINS)
        mask = jnp.concatenate(
            [mask_rows[pl.ds(2 * m, 1), :], mask_rows[pl.ds(2 * m + 1, 1), :]], axis=1
        )
        whitened = spectrum * (mask * lax.rsqrt(smoothed + (0.1 * mean_power + 1e-6)))
        whitened = jnp.where(row == 0, mask, jnp.where(row == 1, 0.0, whitened))
        for u in range(2):
            turned[pl.ds(pl.multiple_of((2 * slot + u) * ROWS, ROWS), ROWS), :] = whitened[
                :, u * LANES : (u + 1) * LANES
            ]

    def send(source, target, size, place_out, place_in, out_sem, in_sem, a, b):
        return pltpu.make_async_remote_copy(
            src_ref=source.at[pl.ds(place_out, size)], dst_ref=target.at[pl.ds(place_in, size)],
            send_sem=out_sem, recv_sem=in_sem, device_id=device(a, b), device_id_type=MESH,
        )

    def far(h, a, b, owner):
        return send(
            send1, recv1, bins, h * BINS + (a * n_tm + b) * bins, h * BINS + owner * bins,
            send1_sem.at[h], recv1_sem.at[h * n + owner], a, b,
        )

    def near(h, a, b, owner):
        return send(
            send1, near1, bins, h * BINS + (((1 - side) * half_a + a) * n_tm + b) * bins,
            (h * (n // 2) + owner) * bins,
            near_send.at[h], near_recv.at[h * (n // 2) + owner], side * half_a + a, b,
        )

    def keep_far(h):
        return pltpu.make_async_copy(
            send1.at[pl.ds(h * BINS + me * bins, bins)],
            recv1.at[pl.ds(h * BINS + me * bins, bins)], local_sem.at[2 + h],
        )

    def keep_near(h):
        return pltpu.make_async_copy(
            send1.at[pl.ds(h * BINS + partner * bins, bins)],
            near1.at[pl.ds((h * (n // 2) + near_me) * bins, bins)], local_sem.at[4 + h],
        )

    fill.wait()
    load.wait()

    def half(h, _):
        def two(p, _):
            @pl.when(jnp.logical_and(h + p == 1, jnp.logical_and(p == 1, has_left)))
            def _():
                to_left.wait_send()
                to_right.wait_recv()

            @pl.when(jnp.logical_and(h + p == 2, has_right))
            def _():
                to_right.wait_send()
                to_left.wait_recv()

            first = jnp.where(h == 0, 1 + 2 * p, 4 + 2 * p)
            second = jnp.where(h == 0, 2 - 2 * p, 5 + 2 * p)
            whiten(first, first - 4 * h)
            whiten(second, second - 4 * h)
            return 0

        lax.fori_loop(0, 2, two, 0)

        def turn(step, _):
            for i in range(8):
                f = step * 8 + i
                tile = jnp.concatenate(
                    [turned[pl.ds(2 * f + c, SUB // 2, stride=ROWS), :] for c in range(2)], axis=0
                )
                send1[h * BINS + f] = tile.astype(jnp.bfloat16)
            return 0

        lax.fori_loop(0, BINS // 8, turn, 0)
        others(chan, n_chan, lambda a, b: far(h, a, b, me).start())
        others(near_chan, half_a, lambda a, b: near(h, a, b, near_me).start())
        keep_far(h).start()
        keep_near(h).start()
        return 0

    lax.fori_loop(0, 2, half, 0)

    lane = lax.broadcasted_iota(jnp.int32, (SUB, LANES), 1)
    low_half = lane < LANES // 2
    even = lax.rem(lane // CHAN_ROWS, 2) == 0
    n_all = n_chan * CHAN_ROWS
    depth = 2 * n_tm * SEGS
    groups = n_chan // PER_LANE

    def swap(first, second, distance, keep):
        return (
            jnp.where(keep, first, pltpu.roll(second, distance, 1)),
            jnp.where(keep, pltpu.roll(first, LANES - distance, 1), second),
        )

    def arrange(tiles, into, width, at, g):
        p0, p2 = swap(tiles[0], tiles[2], 64, low_half)
        p1, p3 = swap(tiles[1], tiles[3], 64, low_half)
        u0, u1 = swap(p0, p1, 32, even)
        u2, u3 = swap(p2, p3, 32, even)
        left = pl.multiple_of(g * LANES, LANES)
        right = pl.multiple_of(width + g * LANES, LANES)
        for q, value in enumerate((u0, u1, u2, u3)):
            rows = pl.ds(pl.multiple_of(at + q * SUB, SUB), SUB)
            other = jnp.concatenate([value[SUB // 2 :], -value[: SUB // 2]], axis=0)
            into[rows, pl.ds(left, LANES)] = value.astype(jnp.bfloat16)
            into[rows, pl.ds(right, LANES)] = other.astype(jnp.bfloat16)

    def gather(h, _):
        keep_far(h).wait()
        keep_near(h).wait()

        def near_group(g, _):
            for b in range(n_tm):
                sources = [(g * PER_LANE + i) * n_tm + b for i in range(PER_LANE)]
                for i, source in enumerate(sources):
                    @pl.when(source != near_me)
                    def _():
                        near(h, g * PER_LANE + i, b, source).wait_recv()

                for f in range(bins):
                    tiles = [
                        near1[(h * (n // 2) + source) * bins + f].astype(jnp.float32)
                        for source in sources
                    ]
                    at = f * depth + (h * n_tm + b) * PER_LANE * SUB
                    arrange(tiles, near_pair, n_half, at, g)
            return 0

        lax.fori_loop(0, groups // 2, near_group, 0)

        def far_group(j, _):
            g = wrap(side * (groups // 2) + j, groups)
            for b in range(n_tm):
                sources = [(g * PER_LANE + i) * n_tm + b for i in range(PER_LANE)]
                for i, source in enumerate(sources):
                    @pl.when(source != me)
                    def _():
                        far(h, g * PER_LANE + i, b, source).wait_recv()

                for f in range(bins):
                    tiles = [
                        recv1[h * BINS + source * bins + f].astype(jnp.float32)
                        for source in sources
                    ]
                    at = f * depth + (h * n_tm + b) * PER_LANE * SUB
                    arrange(tiles, pair, n_all, at, g)
            return 0

        lax.fori_loop(0, groups, far_group, 0)
        return 0

    n_half = n_all // 2
    lax.fori_loop(0, 2, gather, 0)

    paired = upper(tm, half_b) == side
    moved_a, moved_b = wrap(chan + half_a, n_chan), wrap(tm + half_b, n_tm)

    def back(s, a, b):
        slot = a * n_tm + b
        spare = jnp.logical_and(upper(a, half_a) != side, upper(b, half_b) != side)
        to_a = jnp.where(spare, wrap(a + half_a, n_chan), a)
        to_b = jnp.where(spare, wrap(b + half_b, n_tm), b)
        owner = jnp.where(spare, partner, me)
        return send(
            send2, out_hbm, 2 * piece, (slot * bins + s * piece) * 2,
            (owner * bins + s * piece) * 2, send2_sem.at[0], recv2_sem.at[0], to_a, to_b,
        )

    def keep_back(s):
        return pltpu.make_async_copy(
            send2.at[pl.ds((me * bins + s * piece) * 2, 2 * piece)],
            out_hbm.at[pl.ds((me * bins + s * piece) * 2, 2 * piece)], local_sem.at[8 + 2 * s],
        )

    def keep_spare(s):
        slot = moved_a * n_tm + moved_b
        return pltpu.make_async_copy(
            send2.at[pl.ds((slot * bins + s * piece) * 2, 2 * piece)],
            out_hbm.at[pl.ds((partner * bins + s * piece) * 2, 2 * piece)],
            local_sem.at[9 + 2 * s],
        )

    def some_bins(s, _):
        for i in range(piece):
            at = pl.ds(pl.multiple_of((s * piece + i) * depth, depth), depth)
            cross[i] = mm(pair[at, :n_all], pair[at, :], TN)
            near_cross[i] = mm(near_pair[at, :n_half], near_pair[at, :], TN)

        def pack(block, width, i, row, lane_block, owner, slot_a, slot_b):
            f = s * piece + i
            at = pl.multiple_of(row * CHAN_ROWS, CHAN_ROWS)
            tops = []
            for c in range(2):
                lanes = pl.ds(pl.multiple_of(c * width + lane_block * LANES, LANES), LANES)
                top = block[i, pl.ds(at, SUB), lanes]
                bottom = block[i, pl.ds(at + SUB, SUB), lanes]
                tops.append(swap(top, bottom, 64, low_half))
            for e in range(2):
                dest = ((slot_a * n_tm + slot_b + e) * bins + f) * 2
                real = tops[0][e].astype(jnp.bfloat16)
                imag = tops[1][e]
                if i == 0:
                    rest = tops[0][e] - real.astype(jnp.float32)
                    imag = jnp.where(jnp.logical_and(owner == 0, f == 0), rest, imag)
                send2[dest] = real
                send2[dest + 1] = imag.astype(jnp.bfloat16)

        for i in range(piece):
            for k in range(half_a):
                mine, outer = side * half_a + k, (1 - side) * half_a + k
                for p in range(n_tm // 2):
                    pack(cross, n_all, i, mine, p, me, mine, 2 * p)
                for p in range(half_b // 2):
                    inside = side * (half_b // 2) + p
                    pack(cross, n_all, i, outer, inside, me, outer, 2 * inside)
                    pack(
                        near_cross, n_half, i, k, p, partner, outer,
                        (1 - side) * half_b + 2 * p,
                    )

        def one(a, b):
            @pl.when(jnp.logical_not(
                jnp.logical_and(paired, jnp.logical_and(a == moved_a, b == moved_b))
            ))
            def _():
                back(s, a, b).start()

        others(chan, n_chan, one)
        keep_back(s).start()

        @pl.when(paired)
        def _():
            keep_spare(s).start()

        return 0

    lax.fori_loop(0, pieces, some_bins, 0)

    for p in range(pieces):
        keep_back(p).wait()

        @pl.when(paired)
        def _():
            keep_spare(p).wait()

    def all_back(count):
        size = count * 2 * bins
        whole = send(
            send2, out_hbm, size, 0, 0, send2_sem.at[0], recv2_sem.at[0], moved_a, moved_b
        )
        whole.wait_recv()
        whole.wait_send()

    @pl.when(paired)
    def _():
        all_back(n - 2)

    @pl.when(jnp.logical_not(paired))
    def _():
        all_back(n - 1)

    for h in range(2):
        send(
            send1, recv1, (n - 1) * bins, 0, 0, send1_sem.at[h], recv1_sem.at[0], moved_a, moved_b
        ).wait_send()
        send(
            send1, near1, (n // 2 - 1) * bins, 0, 0, near_send.at[h], near_recv.at[0],
            moved_a, moved_b,
        ).wait_send()


def lag_kernel(steps, cross_ref, inverse_ref, out_ref, rows, scale):
    step = pl.program_id(0)

    @pl.when(step == 0)
    def _():
        count = cross_ref[0].astype(jnp.float32) + cross_ref[1].astype(jnp.float32)
        scale[...] = (2.0 / jnp.maximum(count, 1.0)).T

        def turn(block, _):
            for i in range(16):
                r = block * 16 + i
                rows[pl.ds(r, SUB, stride=ROWS), :] = cross_ref[r].astype(jnp.float32)
            return 0

        lax.fori_loop(0, ROWS // 16, turn, 0)

    column = lax.broadcasted_iota(jnp.int32, (LANES, SUB), 1)
    for i in range(SUB // steps):
        index = step * (SUB // steps) + i
        value = rows[pl.ds(pl.multiple_of(index * ROWS, ROWS), ROWS), :].astype(jnp.bfloat16)
        lagged = mm(value, inverse_ref[:ROWS], TN) + mm(value, inverse_ref[ROWS:], TN)
        lagged = lagged * jnp.sum(
            jnp.where(column == index, scale[...], 0.0), axis=1, keepdims=True
        )
        out_ref[0, i] = lagged[: LANES // 2]
        out_ref[1, i] = lagged[LANES // 2 :]


def body(n_chan, n_tm, traces, live_channel, valid_segment):
    forward, inverse, smooth, box = make_tables()
    n = n_chan * n_tm
    n_all = n_chan * CHAN_ROWS
    bins = BINS // n
    piece = min(2, bins)
    pieces = bins // piece
    span = traces.shape[1]
    tables = np.concatenate([*forward, smooth, box], axis=0)
    inverse = np.concatenate(inverse, axis=0)
    hbm = pl.BlockSpec(memory_space=pltpu.HBM)
    dma = pltpu.SemaphoreType.DMA
    tiles = (ROWS, SUB, LANES)
    crossed = pl.pallas_call(
        functools.partial(spread_kernel, n_chan, n_tm, piece),
        out_shape=jax.ShapeDtypeStruct(tiles, jnp.bfloat16),
        in_specs=[hbm] * 4,
        out_specs=hbm,
        scratch_shapes=[
            pltpu.VMEM((1, CHAN_ROWS), jnp.int32),
            pltpu.VMEM((CHAN_ROWS, SEGS), jnp.int32),
            pltpu.VMEM((CHAN_ROWS, span + 2 * LANES), jnp.float32),
            pltpu.VMEM(tables.shape, jnp.bfloat16),
            pltpu.VMEM((SUB, LANES), jnp.float32),
            pltpu.VMEM((SUB // 2 * ROWS, LANES), jnp.float32),
            pltpu.VMEM(tiles, jnp.bfloat16),
            pltpu.VMEM(tiles, jnp.bfloat16),
            pltpu.VMEM((BINS, SUB, LANES), jnp.bfloat16),
            pltpu.VMEM((bins * 2 * n_tm * SEGS, 2 * n_all), jnp.bfloat16),
            pltpu.VMEM((bins * 2 * n_tm * SEGS, n_all), jnp.bfloat16),
            pltpu.VMEM((piece, n_all, 2 * n_all), jnp.float32),
            pltpu.VMEM((piece, n_all // 2, n_all), jnp.float32),
            pltpu.VMEM(tiles, jnp.bfloat16),
            dma((2,)), dma((2,)), dma((8 + 2 * pieces,)),
            dma((2,)), dma((2 * n,)), dma((2,)), dma((n,)), dma((1,)), dma((1,)),
        ],
        compiler_params=pltpu.CompilerParams(
            collective_id=0, has_side_effects=True, vmem_limit_bytes=VMEM_LIMIT
        ),
        name="spread",
    )(traces, tables, live_channel.reshape(1, CHAN_ROWS), valid_segment)
    steps = 4
    lagged = pl.pallas_call(
        functools.partial(lag_kernel, steps),
        out_shape=jax.ShapeDtypeStruct((2, SUB, LANES // 2, SEG_LEN), jnp.float32),
        grid=(steps,),
        in_specs=[
            pl.BlockSpec(tiles, lambda i: (0, 0, 0)),
            pl.BlockSpec((2 * ROWS, SEG_LEN), lambda i: (0, 0)),
        ],
        out_specs=pl.BlockSpec((2, SUB // steps, LANES // 2, SEG_LEN), lambda i: (0, i, 0, 0)),
        scratch_shapes=[
            pltpu.VMEM((SUB * ROWS, LANES), jnp.float32),
            pltpu.VMEM((LANES, SUB), jnp.float32),
        ],
        compiler_params=pltpu.CompilerParams(vmem_limit_bytes=VMEM_LIMIT),
        name="lags",
    )(crossed, inverse)
    return lagged.reshape(CHAN_ROWS, LANES // 2, SEG_LEN)


def solution(mesh):
    n_chan, n_tm = mesh.shape["chan"], mesh.shape["tm"]
    return jax.shard_map(
        functools.partial(body, n_chan, n_tm),
        mesh=mesh,
        in_specs=(P("chan", "tm"), P("chan"), P("chan", "tm")),
        out_specs=P("chan", "tm", None),
        check_vma=False,
    )
```

```python
import functools

import jax
import jax.numpy as jnp
import numpy as np
from jax import lax
from jax.experimental import pallas as pl
from jax.experimental.pallas import tpu as pltpu
from jax.sharding import PartitionSpec as P

SEG_LEN = 256
BINS = 128
HALF_WIN = 64
SMOOTH = 4
ROWS = 2 * BINS
LANES = 128
STRIDE = ROWS + 8
SUB = 16
CHAN_ROWS = 32
SEGS = 64
PER_LANE = LANES // CHAN_ROWS
MESH = pl.DeviceIdType.MESH
VMEM_LIMIT = 63 * 1024 * 1024


def split_table(table):
    high = table.astype(jnp.bfloat16)
    low = (table - high.astype(np.float32)).astype(jnp.bfloat16)
    return high, low


def make_tables():
    row_bin = np.arange(ROWS) // 2
    row_imag = np.arange(ROWS) % 2 == 1
    time = np.arange(SEG_LEN)
    phase = 2.0 * np.pi / SEG_LEN * (row_bin[:, None] * time[None, :] % SEG_LEN)
    forward = np.where(row_imag[:, None], -np.sin(phase), np.cos(phase)).astype(np.float32)
    lag = np.arange(SEG_LEN) - BINS
    back = 2.0 * np.pi / SEG_LEN * (row_bin[:, None] * lag[None, :] % SEG_LEN)
    inverse = np.where(row_imag[:, None], -np.sin(back), np.cos(back))
    inverse = (inverse * (row_bin > 0)[:, None]).astype(np.float32)
    smooth = np.abs(row_bin[:, None] - row_bin[None, :]) <= SMOOTH
    sample_in = np.arange(2 * SEG_LEN)[:, None] - SEG_LEN // 2
    sample_out = np.arange(SEG_LEN)[None, :]
    box = np.abs(sample_in - sample_out) <= HALF_WIN
    return (
        split_table(forward),
        split_table(inverse),
        smooth.astype(jnp.bfloat16),
        box.astype(jnp.bfloat16),
    )


def halves(value):
    high = value.astype(jnp.bfloat16)
    return high, (value - high.astype(jnp.float32)).astype(jnp.bfloat16)


def mm(a, b, dims=((1,), (0,))):
    return lax.dot_general(a, b, (dims, ((), ())), preferred_element_type=jnp.float32)


NT = ((1,), (1,))
TN = ((0,), (0,))


def spread_kernel(
    n_chan, n_tm, piece,
    x_hbm, table_hbm, live_hbm, valid_hbm,
    out_hbm,
    live_ref, valid_ref, xpad, tables, mask_rows, turned, send1, recv1, near1, pair, near_pair, cross, near_cross, send2,
    halo_send, halo_recv, local_sem, send1_sem, recv1_sem, near_send, near_recv, send2_sem, recv2_sem,
):
    n = n_chan * n_tm
    span = SEGS * SEG_LEN
    bins = BINS // n
    pieces = bins // piece
    chan, tm = lax.axis_index("chan"), lax.axis_index("tm")
    me = chan * n_tm + tm
    half_a, half_b = n_chan // 2, n_tm // 2

    def wrap(index, count):
        return jnp.where(index >= count, index - count, index)

    def upper(index, half):
        return (index >= half).astype(jnp.int32)

    side = upper(chan, half_a)
    near_chan = chan - side * half_a
    near_me = near_chan * n_tm + tm
    partner = wrap(chan + half_a, n_chan) * n_tm + tm

    def device(a, b):
        return {"chan": a, "tm": b}

    def others(first, count, act):
        for j in range(1, n_tm):
            act(first, wrap(tm + j, n_tm))

        def one(i, _):
            for j in range(n_tm):
                act(wrap(first + i, count), wrap(tm + j, n_tm))
            return 0

        lax.fori_loop(1, count, one, 0)

    live_in = pltpu.make_async_copy(live_hbm, live_ref, local_sem.at[6])
    live_in.start()
    valid_in = pltpu.make_async_copy(valid_hbm, valid_ref, local_sem.at[7])
    valid_in.start()
    load = pltpu.make_async_copy(table_hbm, tables, local_sem.at[1])
    load.start()
    part = 8 * SEG_LEN
    cuts = (part - LANES, 3 * part + LANES)
    fills = [
        pltpu.make_async_copy(
            x_hbm.at[:, pl.ds(low, high - low)], xpad.at[:, pl.ds(LANES + low, high - low)],
            local_sem.at[sem],
        )
        for sem, low, high in ((0, *cuts), (8 + 2 * pieces, cuts[1], span), (9 + 2 * pieces, 0, cuts[0]))
    ]
    for fill in fills:
        fill.start()

    barrier = pltpu.get_barrier_semaphore()

    others(
        chan, n_chan,
        lambda a, b: pl.semaphore_signal(
            barrier, inc=1, device_id=device(a, b), device_id_type=MESH
        ),
    )

    to_left = pltpu.make_async_remote_copy(
        src_ref=x_hbm.at[:, pl.ds(0, LANES)],
        dst_ref=xpad.at[:, pl.ds(LANES + span, LANES)],
        send_sem=halo_send.at[0], recv_sem=halo_recv.at[0],
        device_id={"chan": chan, "tm": jnp.maximum(tm - 1, 0)}, device_id_type=MESH,
    )
    to_right = pltpu.make_async_remote_copy(
        src_ref=x_hbm.at[:, pl.ds(span - LANES, LANES)],
        dst_ref=xpad.at[:, pl.ds(0, LANES)],
        send_sem=halo_send.at[1], recv_sem=halo_recv.at[1],
        device_id={"chan": chan, "tm": jnp.minimum(tm + 1, n_tm - 1)}, device_id_type=MESH,
    )
    has_left, has_right = tm > 0, tm < n_tm - 1

    @pl.when(jnp.logical_not(has_left))
    def _():
        xpad[:, 0:LANES] = jnp.zeros((CHAN_ROWS, LANES), jnp.float32)

    @pl.when(jnp.logical_not(has_right))
    def _():
        xpad[:, LANES + span : 2 * LANES + span] = jnp.zeros((CHAN_ROWS, LANES), jnp.float32)

    live_in.wait()
    valid_in.wait()
    valid = valid_ref[...].astype(jnp.float32).astype(jnp.bfloat16)
    live = live_ref[...].astype(jnp.float32)
    mask_sum = jnp.zeros((SUB, LANES), jnp.float32)
    seg_row = lax.broadcasted_iota(jnp.int32, (SUB, SEGS), 0) * PER_LANE
    seg_col = lax.broadcasted_iota(jnp.int32, (SUB, SEGS), 1)
    chan_row = lax.broadcasted_iota(jnp.int32, (CHAN_ROWS, LANES), 0)
    chan_lane = lax.broadcasted_iota(jnp.int32, (CHAN_ROWS, LANES), 1)
    for q in range(PER_LANE):
        pick = (seg_col == seg_row + q).astype(jnp.float32).astype(jnp.bfloat16)
        place = (chan_lane == chan_row + q * CHAN_ROWS).astype(jnp.float32).astype(jnp.bfloat16)
        picked = (mm(pick, valid, NT) * live).astype(jnp.bfloat16)
        mask_sum = mask_sum + mm(picked, place)
    mask_rows[...] = mask_sum

    row = lax.broadcasted_iota(jnp.int32, (ROWS, 2 * LANES), 0)

    def whiten(m, slot):
        window = jnp.concatenate(
            [
                xpad[:, pl.ds(pl.multiple_of(m * 8 * SEG_LEN + i * SEG_LEN, LANES), 2 * SEG_LEN)]
                for i in range(8)
            ],
            axis=0,
        )
        box = tables[3 * ROWS : 5 * ROWS]
        high, low = halves(jnp.abs(window))
        level = (mm(high, box) + mm(low, box)) * (1.0 / (2 * HALF_WIN + 1))
        normed = window[:, SEG_LEN // 2 : SEG_LEN // 2 + SEG_LEN] / (level + 1e-5)
        high, low = halves(normed)
        fwd_hi = tables[0:ROWS]
        spectrum = mm(fwd_hi, high, NT) + mm(fwd_hi, low, NT) + mm(tables[ROWS : 2 * ROWS], high, NT)
        power = spectrum * spectrum
        high, low = halves(power)
        smooth = tables[2 * ROWS : 3 * ROWS]
        smoothed = (mm(smooth, high) + mm(smooth, low)) * (1.0 / (2 * SMOOTH + 1))
        mean_power = jnp.sum(power, axis=0, keepdims=True) * (1.0 / BINS)
        mask = jnp.concatenate(
            [mask_rows[pl.ds(2 * m, 1), :], mask_rows[pl.ds(2 * m + 1, 1), :]], axis=1
        )
        whitened = spectrum * (mask * lax.rsqrt(smoothed + (0.1 * mean_power + 1e-6)))
        whitened = jnp.where(row == 0, mask, jnp.where(row == 1, 0.0, whitened))
        for u in range(2):
            at = (2 * slot + u) * STRIDE
            turned[at : at + ROWS, :] = whitened[:, u * LANES : (u + 1) * LANES]

    def send(source, target, size, place_out, place_in, out_sem, in_sem, a, b):
        return pltpu.make_async_remote_copy(
            src_ref=source.at[pl.ds(place_out, size)], dst_ref=target.at[pl.ds(place_in, size)],
            send_sem=out_sem, recv_sem=in_sem, device_id=device(a, b), device_id_type=MESH,
        )

    def far(h, a, b, owner):
        return send(
            send1, recv1, bins, h * BINS + (a * n_tm + b) * bins, h * BINS + owner * bins,
            send1_sem.at[h], recv1_sem.at[h * n + owner], a, b,
        )

    def near(h, a, b, owner):
        return send(
            send1, near1, bins, h * BINS + (((1 - side) * half_a + a) * n_tm + b) * bins,
            (h * (n // 2) + owner) * bins,
            near_send.at[h], near_recv.at[h * (n // 2) + owner], side * half_a + a, b,
        )

    def keep_far(h):
        return pltpu.make_async_copy(
            send1.at[pl.ds(h * BINS + me * bins, bins)],
            recv1.at[pl.ds(h * BINS + me * bins, bins)], local_sem.at[2 + h],
        )

    def keep_near(h):
        return pltpu.make_async_copy(
            send1.at[pl.ds(h * BINS + partner * bins, bins)],
            near1.at[pl.ds((h * (n // 2) + near_me) * bins, bins)], local_sem.at[4 + h],
        )

    load.wait()
    fills[0].wait()
    whiten(1, 0)
    whiten(2, 1)
    pl.semaphore_wait(barrier, n - 1)

    @pl.when(has_left)
    def _():
        to_left.start()

    @pl.when(has_right)
    def _():
        to_right.start()

    fills[1].wait()
    fills[2].wait()

    def half(h, _):
        @pl.when(h == 1)
        def _():
            whiten(5, 0)
            whiten(6, 1)

            @pl.when(has_left)
            def _():
                to_left.wait_send()
                to_right.wait_recv()

            @pl.when(has_right)
            def _():
                to_right.wait_send()
                to_left.wait_recv()

        whiten(jnp.where(h == 0, 3, 0), 2)
        whiten(jnp.where(h == 0, 4, 7), 3)

        def turn(step, _):
            for i in range(8):
                f = step * 8 + i
                tile = jnp.concatenate(
                    [turned[pl.ds(2 * f + c, SUB // 2, stride=STRIDE), :] for c in range(2)], axis=0
                )
                send1[h * BINS + f] = tile.astype(jnp.bfloat16)
            return 0

        lax.fori_loop(0, BINS // 8, turn, 0)
        others(chan, n_chan, lambda a, b: far(h, a, b, me).start())
        others(near_chan, half_a, lambda a, b: near(h, a, b, near_me).start())
        keep_far(h).start()
        keep_near(h).start()
        return 0

    lax.fori_loop(0, 2, half, 0)

    lane = lax.broadcasted_iota(jnp.int32, (SUB, LANES), 1)
    low_half = lane < LANES // 2
    even = lax.rem(lane // CHAN_ROWS, 2) == 0
    n_all = n_chan * CHAN_ROWS
    depth = 2 * n_tm * SEGS
    groups = n_chan // PER_LANE

    def swap(first, second, distance, keep):
        return (
            jnp.where(keep, first, pltpu.roll(second, distance, 1)),
            jnp.where(keep, pltpu.roll(first, LANES - distance, 1), second),
        )

    def arrange(tiles, into, width, at, g):
        p0, p2 = swap(tiles[0], tiles[2], 64, low_half)
        p1, p3 = swap(tiles[1], tiles[3], 64, low_half)
        u0, u1 = swap(p0, p1, 32, even)
        u2, u3 = swap(p2, p3, 32, even)
        left = pl.multiple_of(g * LANES, LANES)
        right = pl.multiple_of(width + g * LANES, LANES)
        for q, value in enumerate((u0, u1, u2, u3)):
            rows = pl.ds(pl.multiple_of(at + q * SUB, SUB), SUB)
            other = jnp.concatenate([value[SUB // 2 :], -value[: SUB // 2]], axis=0)
            into[rows, pl.ds(left, LANES)] = value.astype(jnp.bfloat16)
            into[rows, pl.ds(right, LANES)] = other.astype(jnp.bfloat16)

    def gather(h, _):
        keep_far(h).wait()
        keep_near(h).wait()

        def near_group(g, _):
            for b in range(n_tm):
                sources = [(g * PER_LANE + i) * n_tm + b for i in range(PER_LANE)]
                for i, source in enumerate(sources):
                    @pl.when(source != near_me)
                    def _():
                        near(h, g * PER_LANE + i, b, source).wait_recv()

                for f in range(bins):
                    tiles = [
                        near1[(h * (n // 2) + source) * bins + f].astype(jnp.float32)
                        for source in sources
                    ]
                    at = f * depth + (h * n_tm + b) * PER_LANE * SUB
                    arrange(tiles, near_pair, n_half, at, g)
            return 0

        lax.fori_loop(0, groups // 2, near_group, 0)

        def far_group(j, _):
            g = wrap(side * (groups // 2) + j, groups)
            for b in range(n_tm):
                sources = [(g * PER_LANE + i) * n_tm + b for i in range(PER_LANE)]
                for i, source in enumerate(sources):
                    @pl.when(source != me)
                    def _():
                        far(h, g * PER_LANE + i, b, source).wait_recv()

                for f in range(bins):
                    tiles = [
                        recv1[h * BINS + source * bins + f].astype(jnp.float32)
                        for source in sources
                    ]
                    at = f * depth + (h * n_tm + b) * PER_LANE * SUB
                    arrange(tiles, pair, n_all, at, g)
            return 0

        lax.fori_loop(0, groups, far_group, 0)
        return 0

    n_half = n_all // 2
    lax.fori_loop(0, 2, gather, 0)

    paired = upper(tm, half_b) == side
    moved_a, moved_b = wrap(chan + half_a, n_chan), wrap(tm + half_b, n_tm)

    def back(s, a, b):
        slot = a * n_tm + b
        spare = jnp.logical_and(upper(a, half_a) != side, upper(b, half_b) != side)
        to_a = jnp.where(spare, wrap(a + half_a, n_chan), a)
        to_b = jnp.where(spare, wrap(b + half_b, n_tm), b)
        owner = jnp.where(spare, partner, me)
        return send(
            send2, out_hbm, 2 * piece, (slot * bins + s * piece) * 2,
            (owner * bins + s * piece) * 2, send2_sem.at[0], recv2_sem.at[0], to_a, to_b,
        )

    def keep_back(s):
        return pltpu.make_async_copy(
            send2.at[pl.ds((me * bins + s * piece) * 2, 2 * piece)],
            out_hbm.at[pl.ds((me * bins + s * piece) * 2, 2 * piece)], local_sem.at[8 + 2 * s],
        )

    def keep_spare(s):
        slot = moved_a * n_tm + moved_b
        return pltpu.make_async_copy(
            send2.at[pl.ds((slot * bins + s * piece) * 2, 2 * piece)],
            out_hbm.at[pl.ds((partner * bins + s * piece) * 2, 2 * piece)],
            local_sem.at[9 + 2 * s],
        )

    def some_bins(s, _):
        for i in range(piece):
            at = pl.ds(pl.multiple_of((s * piece + i) * depth, depth), depth)
            cross[i] = mm(pair[at, :n_all], pair[at, :], TN)
            near_cross[i] = mm(near_pair[at, :n_half], near_pair[at, :], TN)

        def pack(block, width, i, row, lane_block, owner, slot_a, slot_b):
            f = s * piece + i
            at = pl.multiple_of(row * CHAN_ROWS, CHAN_ROWS)
            tops = []
            for c in range(2):
                lanes = pl.ds(pl.multiple_of(c * width + lane_block * LANES, LANES), LANES)
                top = block[i, pl.ds(at, SUB), lanes]
                bottom = block[i, pl.ds(at + SUB, SUB), lanes]
                tops.append(swap(top, bottom, 64, low_half))
            for e in range(2):
                dest = ((slot_a * n_tm + slot_b + e) * bins + f) * 2
                real = tops[0][e].astype(jnp.bfloat16)
                imag = tops[1][e]
                if i == 0:
                    rest = tops[0][e] - real.astype(jnp.float32)
                    imag = jnp.where(jnp.logical_and(owner == 0, f == 0), rest, imag)
                send2[dest] = real
                send2[dest + 1] = imag.astype(jnp.bfloat16)

        for i in range(piece):
            for k in range(half_a):
                mine, outer = side * half_a + k, (1 - side) * half_a + k
                for p in range(n_tm // 2):
                    pack(cross, n_all, i, mine, p, me, mine, 2 * p)
                for p in range(half_b // 2):
                    inside = side * (half_b // 2) + p
                    pack(cross, n_all, i, outer, inside, me, outer, 2 * inside)
                    pack(
                        near_cross, n_half, i, k, p, partner, outer,
                        (1 - side) * half_b + 2 * p,
                    )

        def one(a, b):
            @pl.when(jnp.logical_not(
                jnp.logical_and(paired, jnp.logical_and(a == moved_a, b == moved_b))
            ))
            def _():
                back(s, a, b).start()

        others(chan, n_chan, one)
        keep_back(s).start()

        @pl.when(paired)
        def _():
            keep_spare(s).start()

        return 0

    lax.fori_loop(0, pieces, some_bins, 0)

    for p in range(pieces):
        keep_back(p).wait()

        @pl.when(paired)
        def _():
            keep_spare(p).wait()

    def all_back(count):
        size = count * 2 * bins
        whole = send(
            send2, out_hbm, size, 0, 0, send2_sem.at[0], recv2_sem.at[0], moved_a, moved_b
        )
        whole.wait_recv()
        whole.wait_send()

    @pl.when(paired)
    def _():
        all_back(n - 2)

    @pl.when(jnp.logical_not(paired))
    def _():
        all_back(n - 1)

    for h in range(2):
        send(
            send1, recv1, (n - 1) * bins, 0, 0, send1_sem.at[h], recv1_sem.at[0], moved_a, moved_b
        ).wait_send()
        send(
            send1, near1, (n // 2 - 1) * bins, 0, 0, near_send.at[h], near_recv.at[0],
            moved_a, moved_b,
        ).wait_send()


def lag_kernel(steps, cross_ref, inverse_ref, out_ref, rows, scale):
    step = pl.program_id(0)

    @pl.when(step == 0)
    def _():
        count = cross_ref[0].astype(jnp.float32) + cross_ref[1].astype(jnp.float32)
        scale[...] = (2.0 / jnp.maximum(count, 1.0)).T

        def turn(block, _):
            for i in range(16):
                r = block * 16 + i
                rows[pl.ds(r, SUB, stride=STRIDE), :] = cross_ref[r].astype(jnp.float32)
            return 0

        lax.fori_loop(0, ROWS // 16, turn, 0)

    column = lax.broadcasted_iota(jnp.int32, (LANES, SUB), 1)
    for i in range(SUB // steps):
        index = step * (SUB // steps) + i
        value = rows[pl.ds(pl.multiple_of(index * STRIDE, 8), ROWS), :].astype(jnp.bfloat16)
        lagged = mm(value, inverse_ref[:ROWS], TN) + mm(value, inverse_ref[ROWS:], TN)
        lagged = lagged * jnp.sum(
            jnp.where(column == index, scale[...], 0.0), axis=1, keepdims=True
        )
        out_ref[0, i] = lagged[: LANES // 2]
        out_ref[1, i] = lagged[LANES // 2 :]


def body(n_chan, n_tm, traces, live_channel, valid_segment):
    forward, inverse, smooth, box = make_tables()
    n = n_chan * n_tm
    n_all = n_chan * CHAN_ROWS
    bins = BINS // n
    piece = min(2, bins)
    pieces = bins // piece
    span = traces.shape[1]
    tables = np.concatenate([*forward, smooth, box], axis=0)
    inverse = np.concatenate(inverse, axis=0)
    hbm = pl.BlockSpec(memory_space=pltpu.HBM)
    dma = pltpu.SemaphoreType.DMA
    tiles = (ROWS, SUB, LANES)
    crossed = pl.pallas_call(
        functools.partial(spread_kernel, n_chan, n_tm, piece),
        out_shape=jax.ShapeDtypeStruct(tiles, jnp.bfloat16),
        in_specs=[hbm] * 4,
        out_specs=hbm,
        scratch_shapes=[
            pltpu.VMEM((1, CHAN_ROWS), jnp.int32),
            pltpu.VMEM((CHAN_ROWS, SEGS), jnp.int32),
            pltpu.VMEM((CHAN_ROWS, span + 2 * LANES), jnp.float32),
            pltpu.VMEM(tables.shape, jnp.bfloat16),
            pltpu.VMEM((SUB, LANES), jnp.float32),
            pltpu.VMEM((SUB // 2 * STRIDE, LANES), jnp.float32),
            pltpu.VMEM(tiles, jnp.bfloat16),
            pltpu.VMEM(tiles, jnp.bfloat16),
            pltpu.VMEM((BINS, SUB, LANES), jnp.bfloat16),
            pltpu.VMEM((bins * 2 * n_tm * SEGS, 2 * n_all), jnp.bfloat16),
            pltpu.VMEM((bins * 2 * n_tm * SEGS, n_all), jnp.bfloat16),
            pltpu.VMEM((piece, n_all, 2 * n_all), jnp.float32),
            pltpu.VMEM((piece, n_all // 2, n_all), jnp.float32),
            pltpu.VMEM(tiles, jnp.bfloat16),
            dma((2,)), dma((2,)), dma((10 + 2 * pieces,)),
            dma((2,)), dma((2 * n,)), dma((2,)), dma((n,)), dma((1,)), dma((1,)),
        ],
        compiler_params=pltpu.CompilerParams(
            collective_id=0, has_side_effects=True, vmem_limit_bytes=VMEM_LIMIT
        ),
        name="spread",
    )(traces, tables, live_channel.reshape(1, CHAN_ROWS), valid_segment)
    steps = 4
    lagged = pl.pallas_call(
        functools.partial(lag_kernel, steps),
        out_shape=jax.ShapeDtypeStruct((2, SUB, LANES // 2, SEG_LEN), jnp.float32),
        grid=(steps,),
        in_specs=[
            pl.BlockSpec(tiles, lambda i: (0, 0, 0)),
            pl.BlockSpec((2 * ROWS, SEG_LEN), lambda i: (0, 0)),
        ],
        out_specs=pl.BlockSpec((2, SUB // steps, LANES // 2, SEG_LEN), lambda i: (0, i, 0, 0)),
        scratch_shapes=[
            pltpu.VMEM((SUB * STRIDE, LANES), jnp.float32),
            pltpu.VMEM((LANES, SUB), jnp.float32),
        ],
        compiler_params=pltpu.CompilerParams(vmem_limit_bytes=VMEM_LIMIT),
        name="lags",
    )(crossed, inverse)
    return lagged.reshape(CHAN_ROWS, LANES // 2, SEG_LEN)


def solution(mesh):
    n_chan, n_tm = mesh.shape["chan"], mesh.shape["tm"]
    return jax.shard_map(
        functools.partial(body, n_chan, n_tm),
        mesh=mesh,
        in_specs=(P("chan", "tm"), P("chan"), P("chan", "tm")),
        out_specs=P("chan", "tm", None),
        check_vma=False,
    )
```

```python
import functools

import jax
import jax.numpy as jnp
import numpy as np
from jax import lax
from jax.experimental import pallas as pl
from jax.experimental.pallas import tpu as pltpu
from jax.sharding import PartitionSpec as P

SEG_LEN = 256
BINS = 128
HALF_WIN = 64
SMOOTH = 4
ROWS = 2 * BINS
LANES = 128
STRIDE = ROWS + 8
SUB = 16
CHAN_ROWS = 32
SEGS = 64
PER_LANE = LANES // CHAN_ROWS
MESH = pl.DeviceIdType.MESH
VMEM_LIMIT = 63 * 1024 * 1024


def split_table(table):
    high = table.astype(jnp.bfloat16)
    low = (table - high.astype(np.float32)).astype(jnp.bfloat16)
    return high, low


def make_tables():
    row_bin = np.arange(ROWS) // 2
    row_imag = np.arange(ROWS) % 2 == 1
    time = np.arange(SEG_LEN)
    phase = 2.0 * np.pi / SEG_LEN * (row_bin[:, None] * time[None, :] % SEG_LEN)
    forward = np.where(row_imag[:, None], -np.sin(phase), np.cos(phase)).astype(np.float32)
    lag = np.arange(SEG_LEN) - BINS
    back = 2.0 * np.pi / SEG_LEN * (row_bin[:, None] * lag[None, :] % SEG_LEN)
    inverse = np.where(row_imag[:, None], -np.sin(back), np.cos(back))
    inverse = (inverse * (row_bin > 0)[:, None]).astype(np.float32)
    smooth = np.abs(row_bin[:, None] - row_bin[None, :]) <= SMOOTH
    sample_in = np.arange(2 * SEG_LEN)[:, None] - SEG_LEN // 2
    sample_out = np.arange(SEG_LEN)[None, :]
    box = np.abs(sample_in - sample_out) <= HALF_WIN
    return (
        split_table(forward),
        split_table(inverse),
        smooth.astype(jnp.bfloat16),
        box.astype(jnp.bfloat16),
    )


def halves(value):
    high = value.astype(jnp.bfloat16)
    return high, (value - high.astype(jnp.float32)).astype(jnp.bfloat16)


def mm(a, b, dims=((1,), (0,))):
    return lax.dot_general(a, b, (dims, ((), ())), preferred_element_type=jnp.float32)


NT = ((1,), (1,))
TN = ((0,), (0,))


def spread_kernel(
    n_chan, n_tm, piece,
    x_hbm, table_hbm, live_hbm, valid_hbm,
    out_hbm,
    live_ref, valid_ref, xpad, tables, mask_rows, turned, send1, recv1, near1, pair, near_pair, cross, near_cross, send2,
    halo_send, halo_recv, local_sem, send1_sem, recv1_sem, near_send, near_recv, send2_sem, recv2_sem,
):
    n = n_chan * n_tm
    span = SEGS * SEG_LEN
    bins = BINS // n
    pieces = bins // piece
    chan, tm = lax.axis_index("chan"), lax.axis_index("tm")
    me = chan * n_tm + tm
    half_a, half_b = n_chan // 2, n_tm // 2

    def wrap(index, count):
        return jnp.where(index >= count, index - count, index)

    def upper(index, half):
        return (index >= half).astype(jnp.int32)

    side = upper(chan, half_a)
    near_chan = chan - side * half_a
    near_me = near_chan * n_tm + tm
    partner = wrap(chan + half_a, n_chan) * n_tm + tm

    def device(a, b):
        return {"chan": a, "tm": b}

    def others(first, count, act):
        for j in range(1, n_tm):
            act(first, wrap(tm + j, n_tm))

        def one(i, _):
            for j in range(n_tm):
                act(wrap(first + i, count), wrap(tm + j, n_tm))
            return 0

        lax.fori_loop(1, count, one, 0)

    live_in = pltpu.make_async_copy(live_hbm, live_ref, local_sem.at[6])
    live_in.start()
    valid_in = pltpu.make_async_copy(valid_hbm, valid_ref, local_sem.at[7])
    valid_in.start()
    load = pltpu.make_async_copy(table_hbm, tables, local_sem.at[1])
    load.start()
    part = 8 * SEG_LEN
    cuts = (part - LANES, 3 * part + LANES)
    fills = [
        pltpu.make_async_copy(
            x_hbm.at[:, pl.ds(low, high - low)], xpad.at[:, pl.ds(LANES + low, high - low)],
            local_sem.at[sem],
        )
        for sem, low, high in ((0, *cuts), (8 + 2 * pieces, cuts[1], span), (9 + 2 * pieces, 0, cuts[0]))
    ]
    for fill in fills:
        fill.start()

    barrier = pltpu.get_barrier_semaphore()

    others(
        chan, n_chan,
        lambda a, b: pl.semaphore_signal(
            barrier, inc=1, device_id=device(a, b), device_id_type=MESH
        ),
    )

    to_left = pltpu.make_async_remote_copy(
        src_ref=x_hbm.at[:, pl.ds(0, LANES)],
        dst_ref=xpad.at[:, pl.ds(LANES + span, LANES)],
        send_sem=halo_send.at[0], recv_sem=halo_recv.at[0],
        device_id={"chan": chan, "tm": jnp.maximum(tm - 1, 0)}, device_id_type=MESH,
    )
    to_right = pltpu.make_async_remote_copy(
        src_ref=x_hbm.at[:, pl.ds(span - LANES, LANES)],
        dst_ref=xpad.at[:, pl.ds(0, LANES)],
        send_sem=halo_send.at[1], recv_sem=halo_recv.at[1],
        device_id={"chan": chan, "tm": jnp.minimum(tm + 1, n_tm - 1)}, device_id_type=MESH,
    )
    has_left, has_right = tm > 0, tm < n_tm - 1

    @pl.when(jnp.logical_not(has_left))
    def _():
        xpad[:, 0:LANES] = jnp.zeros((CHAN_ROWS, LANES), jnp.float32)

    @pl.when(jnp.logical_not(has_right))
    def _():
        xpad[:, LANES + span : 2 * LANES + span] = jnp.zeros((CHAN_ROWS, LANES), jnp.float32)

    live_in.wait()
    valid_in.wait()
    valid = valid_ref[...].astype(jnp.float32).astype(jnp.bfloat16)
    live = live_ref[...].astype(jnp.float32)
    mask_sum = jnp.zeros((SUB, LANES), jnp.float32)
    seg_row = lax.broadcasted_iota(jnp.int32, (SUB, SEGS), 0) * PER_LANE
    seg_col = lax.broadcasted_iota(jnp.int32, (SUB, SEGS), 1)
    chan_row = lax.broadcasted_iota(jnp.int32, (CHAN_ROWS, LANES), 0)
    chan_lane = lax.broadcasted_iota(jnp.int32, (CHAN_ROWS, LANES), 1)
    for q in range(PER_LANE):
        pick = (seg_col == seg_row + q).astype(jnp.float32).astype(jnp.bfloat16)
        place = (chan_lane == chan_row + q * CHAN_ROWS).astype(jnp.float32).astype(jnp.bfloat16)
        picked = (mm(pick, valid, NT) * live).astype(jnp.bfloat16)
        mask_sum = mask_sum + mm(picked, place)
    mask_rows[...] = mask_sum

    row = lax.broadcasted_iota(jnp.int32, (ROWS, 2 * LANES), 0)

    def whiten(m, slot):
        window = jnp.concatenate(
            [
                xpad[:, pl.ds(pl.multiple_of(m * 8 * SEG_LEN + i * SEG_LEN, LANES), 2 * SEG_LEN)]
                for i in range(8)
            ],
            axis=0,
        )
        box = tables[3 * ROWS : 5 * ROWS]
        high, low = halves(jnp.abs(window))
        level = (mm(high, box) + mm(low, box)) * (1.0 / (2 * HALF_WIN + 1))
        normed = window[:, SEG_LEN // 2 : SEG_LEN // 2 + SEG_LEN] / (level + 1e-5)
        high, low = halves(normed)
        fwd_hi = tables[0:ROWS]
        spectrum = mm(fwd_hi, high, NT) + mm(fwd_hi, low, NT) + mm(tables[ROWS : 2 * ROWS], high, NT)
        power = spectrum * spectrum
        high, low = halves(power)
        smooth = tables[2 * ROWS : 3 * ROWS]
        smoothed = (mm(smooth, high) + mm(smooth, low)) * (1.0 / (2 * SMOOTH + 1))
        mean_power = jnp.sum(power, axis=0, keepdims=True) * (1.0 / BINS)
        mask = jnp.concatenate(
            [mask_rows[pl.ds(2 * m, 1), :], mask_rows[pl.ds(2 * m + 1, 1), :]], axis=1
        )
        whitened = spectrum * (mask * lax.rsqrt(smoothed + (0.1 * mean_power + 1e-6)))
        whitened = jnp.where(row == 0, mask, jnp.where(row == 1, 0.0, whitened))
        for u in range(2):
            at = (2 * slot + u) * STRIDE
            turned[at : at + ROWS, :] = whitened[:, u * LANES : (u + 1) * LANES]

    def send(source, target, size, place_out, place_in, out_sem, in_sem, a, b):
        return pltpu.make_async_remote_copy(
            src_ref=source.at[pl.ds(place_out, size)], dst_ref=target.at[pl.ds(place_in, size)],
            send_sem=out_sem, recv_sem=in_sem, device_id=device(a, b), device_id_type=MESH,
        )

    def far(h, a, b, owner):
        return send(
            send1, recv1, bins, h * BINS + (a * n_tm + b) * bins, h * BINS + owner * bins,
            send1_sem.at[h], recv1_sem.at[h * n + owner], a, b,
        )

    def near(h, a, b, owner):
        return send(
            send1, near1, bins, h * BINS + (((1 - side) * half_a + a) * n_tm + b) * bins,
            (h * (n // 2) + owner) * bins,
            near_send.at[h], near_recv.at[h * (n // 2) + owner], side * half_a + a, b,
        )

    def keep_far(h):
        return pltpu.make_async_copy(
            send1.at[pl.ds(h * BINS + me * bins, bins)],
            recv1.at[pl.ds(h * BINS + me * bins, bins)], local_sem.at[2 + h],
        )

    def keep_near(h):
        return pltpu.make_async_copy(
            send1.at[pl.ds(h * BINS + partner * bins, bins)],
            near1.at[pl.ds((h * (n // 2) + near_me) * bins, bins)], local_sem.at[4 + h],
        )

    load.wait()
    fills[0].wait()
    whiten(1, 0)
    whiten(2, 1)
    pl.semaphore_wait(barrier, n - 1)

    @pl.when(has_left)
    def _():
        to_left.start()

    @pl.when(has_right)
    def _():
        to_right.start()

    fills[1].wait()
    fills[2].wait()

    def half(h, _):
        @pl.when(h == 1)
        def _():
            whiten(5, 0)
            whiten(6, 1)

            @pl.when(has_left)
            def _():
                to_left.wait_send()
                to_right.wait_recv()

            @pl.when(has_right)
            def _():
                to_right.wait_send()
                to_left.wait_recv()

        whiten(jnp.where(h == 0, 3, 0), 2)
        whiten(jnp.where(h == 0, 4, 7), 3)

        def turn(step, _):
            for i in range(8):
                f = step * 8 + i
                tile = jnp.concatenate(
                    [turned[pl.ds(2 * f + c, SUB // 2, stride=STRIDE), :] for c in range(2)], axis=0
                )
                send1[h * BINS + f] = tile.astype(jnp.bfloat16)
            return 0

        lax.fori_loop(0, BINS // 8, turn, 0)
        others(chan, n_chan, lambda a, b: far(h, a, b, me).start())
        others(near_chan, half_a, lambda a, b: near(h, a, b, near_me).start())
        keep_far(h).start()
        keep_near(h).start()
        return 0

    lax.fori_loop(0, 2, half, 0)

    lane = lax.broadcasted_iota(jnp.int32, (SUB, LANES), 1)
    low_half = lane < LANES // 2
    even = lax.rem(lane // CHAN_ROWS, 2) == 0
    n_all = n_chan * CHAN_ROWS
    depth = 2 * n_tm * SEGS
    groups = n_chan // PER_LANE

    def swap(first, second, distance, keep):
        return (
            jnp.where(keep, first, pltpu.roll(second, distance, 1)),
            jnp.where(keep, pltpu.roll(first, LANES - distance, 1), second),
        )

    def arrange(tiles, into, width, at, g):
        p0, p2 = swap(tiles[0], tiles[2], 64, low_half)
        p1, p3 = swap(tiles[1], tiles[3], 64, low_half)
        u0, u1 = swap(p0, p1, 32, even)
        u2, u3 = swap(p2, p3, 32, even)
        left = pl.multiple_of(g * LANES, LANES)
        right = pl.multiple_of(width + g * LANES, LANES)
        for q, value in enumerate((u0, u1, u2, u3)):
            rows = pl.ds(pl.multiple_of(at + q * SUB, SUB), SUB)
            other = jnp.concatenate([value[SUB // 2 :], -value[: SUB // 2]], axis=0)
            into[rows, pl.ds(left, LANES)] = value.astype(jnp.bfloat16)
            into[rows, pl.ds(right, LANES)] = other.astype(jnp.bfloat16)

    def gather(h, _):
        keep_far(h).wait()
        keep_near(h).wait()

        def near_group(g, _):
            for b in range(n_tm):
                sources = [(g * PER_LANE + i) * n_tm + b for i in range(PER_LANE)]
                for i, source in enumerate(sources):
                    @pl.when(source != near_me)
                    def _():
                        near(h, g * PER_LANE + i, b, source).wait_recv()

                for f in range(bins):
                    tiles = [
                        near1[(h * (n // 2) + source) * bins + f].astype(jnp.float32)
                        for source in sources
                    ]
                    at = f * depth + (h * n_tm + b) * PER_LANE * SUB
                    arrange(tiles, near_pair, n_half, at, g)
            return 0

        def far_group(j, _):
            g = wrap(side * (groups // 2) + j, groups)
            for b in range(n_tm):
                sources = [(g * PER_LANE + i) * n_tm + b for i in range(PER_LANE)]
                for i, source in enumerate(sources):
                    @pl.when(source != me)
                    def _():
                        far(h, g * PER_LANE + i, b, source).wait_recv()

                for f in range(bins):
                    tiles = [
                        recv1[h * BINS + source * bins + f].astype(jnp.float32)
                        for source in sources
                    ]
                    at = f * depth + (h * n_tm + b) * PER_LANE * SUB
                    arrange(tiles, pair, n_all, at, g)
            return 0

        lax.fori_loop(0, groups, far_group, 0)
        lax.fori_loop(0, groups // 2, near_group, 0)
        return 0

    n_half = n_all // 2
    lax.fori_loop(0, 2, gather, 0)

    paired = upper(tm, half_b) == side
    moved_a, moved_b = wrap(chan + half_a, n_chan), wrap(tm + half_b, n_tm)

    def back(s, a, b):
        slot = a * n_tm + b
        spare = jnp.logical_and(upper(a, half_a) != side, upper(b, half_b) != side)
        to_a = jnp.where(spare, wrap(a + half_a, n_chan), a)
        to_b = jnp.where(spare, wrap(b + half_b, n_tm), b)
        owner = jnp.where(spare, partner, me)
        return send(
            send2, out_hbm, 2 * piece, (slot * bins + s * piece) * 2,
            (owner * bins + s * piece) * 2, send2_sem.at[0], recv2_sem.at[0], to_a, to_b,
        )

    def keep_back(s):
        return pltpu.make_async_copy(
            send2.at[pl.ds((me * bins + s * piece) * 2, 2 * piece)],
            out_hbm.at[pl.ds((me * bins + s * piece) * 2, 2 * piece)], local_sem.at[8 + 2 * s],
        )

    def keep_spare(s):
        slot = moved_a * n_tm + moved_b
        return pltpu.make_async_copy(
            send2.at[pl.ds((slot * bins + s * piece) * 2, 2 * piece)],
            out_hbm.at[pl.ds((partner * bins + s * piece) * 2, 2 * piece)],
            local_sem.at[9 + 2 * s],
        )

    def some_bins(s, _):
        for i in range(piece):
            at = pl.ds(pl.multiple_of((s * piece + i) * depth, depth), depth)
            cross[i] = mm(pair[at, :n_all], pair[at, :], TN)
            near_cross[i] = mm(near_pair[at, :n_half], near_pair[at, :], TN)

        def pack(block, width, i, row, lane_block, owner, slot_a, slot_b):
            f = s * piece + i
            at = pl.multiple_of(row * CHAN_ROWS, CHAN_ROWS)
            tops = []
            for c in range(2):
                lanes = pl.ds(pl.multiple_of(c * width + lane_block * LANES, LANES), LANES)
                top = block[i, pl.ds(at, SUB), lanes]
                bottom = block[i, pl.ds(at + SUB, SUB), lanes]
                tops.append(swap(top, bottom, 64, low_half))
            for e in range(2):
                dest = ((slot_a * n_tm + slot_b + e) * bins + f) * 2
                real = tops[0][e].astype(jnp.bfloat16)
                imag = tops[1][e]
                if i == 0:
                    rest = tops[0][e] - real.astype(jnp.float32)
                    imag = jnp.where(jnp.logical_and(owner == 0, f == 0), rest, imag)
                send2[dest] = real
                send2[dest + 1] = imag.astype(jnp.bfloat16)

        for i in range(piece):
            for k in range(half_a):
                mine, outer = side * half_a + k, (1 - side) * half_a + k
                for p in range(n_tm // 2):
                    pack(cross, n_all, i, mine, p, me, mine, 2 * p)
                for p in range(half_b // 2):
                    inside = side * (half_b // 2) + p
                    pack(cross, n_all, i, outer, inside, me, outer, 2 * inside)
                    pack(
                        near_cross, n_half, i, k, p, partner, outer,
                        (1 - side) * half_b + 2 * p,
                    )

        def one(a, b):
            @pl.when(jnp.logical_not(
                jnp.logical_and(paired, jnp.logical_and(a == moved_a, b == moved_b))
            ))
            def _():
                back(s, a, b).start()

        others(chan, n_chan, one)
        keep_back(s).start()

        @pl.when(paired)
        def _():
            keep_spare(s).start()

        return 0

    lax.fori_loop(0, pieces, some_bins, 0)

    for p in range(pieces):
        keep_back(p).wait()

        @pl.when(paired)
        def _():
            keep_spare(p).wait()

    def all_back(count):
        size = count * 2 * bins
        whole = send(
            send2, out_hbm, size, 0, 0, send2_sem.at[0], recv2_sem.at[0], moved_a, moved_b
        )
        whole.wait_recv()
        whole.wait_send()

    @pl.when(paired)
    def _():
        all_back(n - 2)

    @pl.when(jnp.logical_not(paired))
    def _():
        all_back(n - 1)

    for h in range(2):
        send(
            send1, recv1, (n - 1) * bins, 0, 0, send1_sem.at[h], recv1_sem.at[0], moved_a, moved_b
        ).wait_send()
        send(
            send1, near1, (n // 2 - 1) * bins, 0, 0, near_send.at[h], near_recv.at[0],
            moved_a, moved_b,
        ).wait_send()


def lag_kernel(steps, cross_ref, inverse_ref, out_ref, rows, scale):
    step = pl.program_id(0)

    @pl.when(step == 0)
    def _():
        count = cross_ref[0].astype(jnp.float32) + cross_ref[1].astype(jnp.float32)
        scale[...] = (2.0 / jnp.maximum(count, 1.0)).T

        def turn(block, _):
            for i in range(16):
                r = block * 16 + i
                rows[pl.ds(r, SUB, stride=STRIDE), :] = cross_ref[r].astype(jnp.float32)
            return 0

        lax.fori_loop(0, ROWS // 16, turn, 0)

    column = lax.broadcasted_iota(jnp.int32, (LANES, SUB), 1)
    for i in range(SUB // steps):
        index = step * (SUB // steps) + i
        value = rows[pl.ds(pl.multiple_of(index * STRIDE, 8), ROWS), :].astype(jnp.bfloat16)
        lagged = mm(value, inverse_ref[:ROWS], TN) + mm(value, inverse_ref[ROWS:], TN)
        lagged = lagged * jnp.sum(
            jnp.where(column == index, scale[...], 0.0), axis=1, keepdims=True
        )
        out_ref[0, i] = lagged[: LANES // 2]
        out_ref[1, i] = lagged[LANES // 2 :]


def body(n_chan, n_tm, traces, live_channel, valid_segment):
    forward, inverse, smooth, box = make_tables()
    n = n_chan * n_tm
    n_all = n_chan * CHAN_ROWS
    bins = BINS // n
    piece = 1
    pieces = bins // piece
    span = traces.shape[1]
    tables = np.concatenate([*forward, smooth, box], axis=0)
    inverse = np.concatenate(inverse, axis=0)
    hbm = pl.BlockSpec(memory_space=pltpu.HBM)
    dma = pltpu.SemaphoreType.DMA
    tiles = (ROWS, SUB, LANES)
    crossed = pl.pallas_call(
        functools.partial(spread_kernel, n_chan, n_tm, piece),
        out_shape=jax.ShapeDtypeStruct(tiles, jnp.bfloat16),
        in_specs=[hbm] * 4,
        out_specs=hbm,
        scratch_shapes=[
            pltpu.VMEM((1, CHAN_ROWS), jnp.int32),
            pltpu.VMEM((CHAN_ROWS, SEGS), jnp.int32),
            pltpu.VMEM((CHAN_ROWS, span + 2 * LANES), jnp.float32),
            pltpu.VMEM(tables.shape, jnp.bfloat16),
            pltpu.VMEM((SUB, LANES), jnp.float32),
            pltpu.VMEM((SUB // 2 * STRIDE, LANES), jnp.float32),
            pltpu.VMEM(tiles, jnp.bfloat16),
            pltpu.VMEM(tiles, jnp.bfloat16),
            pltpu.VMEM((BINS, SUB, LANES), jnp.bfloat16),
            pltpu.VMEM((bins * 2 * n_tm * SEGS, 2 * n_all), jnp.bfloat16),
            pltpu.VMEM((bins * 2 * n_tm * SEGS, n_all), jnp.bfloat16),
            pltpu.VMEM((piece, n_all, 2 * n_all), jnp.float32),
            pltpu.VMEM((piece, n_all // 2, n_all), jnp.float32),
            pltpu.VMEM(tiles, jnp.bfloat16),
            dma((2,)), dma((2,)), dma((10 + 2 * pieces,)),
            dma((2,)), dma((2 * n,)), dma((2,)), dma((n,)), dma((1,)), dma((1,)),
        ],
        compiler_params=pltpu.CompilerParams(
            collective_id=0, has_side_effects=True, vmem_limit_bytes=VMEM_LIMIT
        ),
        name="spread",
    )(traces, tables, live_channel.reshape(1, CHAN_ROWS), valid_segment)
    steps = 4
    lagged = pl.pallas_call(
        functools.partial(lag_kernel, steps),
        out_shape=jax.ShapeDtypeStruct((2, SUB, LANES // 2, SEG_LEN), jnp.float32),
        grid=(steps,),
        in_specs=[
            pl.BlockSpec(tiles, lambda i: (0, 0, 0)),
            pl.BlockSpec((2 * ROWS, SEG_LEN), lambda i: (0, 0)),
        ],
        out_specs=pl.BlockSpec((2, SUB // steps, LANES // 2, SEG_LEN), lambda i: (0, i, 0, 0)),
        scratch_shapes=[
            pltpu.VMEM((SUB * STRIDE, LANES), jnp.float32),
            pltpu.VMEM((LANES, SUB), jnp.float32),
        ],
        compiler_params=pltpu.CompilerParams(vmem_limit_bytes=VMEM_LIMIT),
        name="lags",
    )(crossed, inverse)
    return lagged.reshape(CHAN_ROWS, LANES // 2, SEG_LEN)


def solution(mesh):
    n_chan, n_tm = mesh.shape["chan"], mesh.shape["tm"]
    return jax.shard_map(
        functools.partial(body, n_chan, n_tm),
        mesh=mesh,
        in_specs=(P("chan", "tm"), P("chan"), P("chan", "tm")),
        out_specs=P("chan", "tm", None),
        check_vma=False,
    )
```

```python
import functools

import jax
import jax.numpy as jnp
import numpy as np
from jax import lax
from jax.experimental import pallas as pl
from jax.experimental.pallas import tpu as pltpu
from jax.sharding import PartitionSpec as P

SEG_LEN = 256
BINS = 128
HALF_WIN = 64
SMOOTH = 4
ROWS = 2 * BINS
LANES = 128
STRIDE = ROWS + 8
SUB = 16
CHAN_ROWS = 32
SEGS = 64
PER_LANE = LANES // CHAN_ROWS
MESH = pl.DeviceIdType.MESH
VMEM_LIMIT = 63 * 1024 * 1024


def split_table(table):
    high = table.astype(jnp.bfloat16)
    low = (table - high.astype(np.float32)).astype(jnp.bfloat16)
    return high, low


def make_tables():
    row_bin = np.arange(ROWS) // 2
    row_imag = np.arange(ROWS) % 2 == 1
    time = np.arange(SEG_LEN)
    phase = 2.0 * np.pi / SEG_LEN * (row_bin[:, None] * time[None, :] % SEG_LEN)
    forward = np.where(row_imag[:, None], -np.sin(phase), np.cos(phase)).astype(np.float32)
    lag = np.arange(SEG_LEN) - BINS
    back = 2.0 * np.pi / SEG_LEN * (row_bin[:, None] * lag[None, :] % SEG_LEN)
    inverse = np.where(row_imag[:, None], -np.sin(back), np.cos(back))
    inverse = (inverse * (row_bin > 0)[:, None]).astype(np.float32)
    smooth = np.abs(row_bin[:, None] - row_bin[None, :]) <= SMOOTH
    sample_in = np.arange(2 * SEG_LEN)[:, None] - SEG_LEN // 2
    sample_out = np.arange(SEG_LEN)[None, :]
    box = np.abs(sample_in - sample_out) <= HALF_WIN
    return (
        split_table(forward),
        split_table(inverse),
        smooth.astype(jnp.bfloat16),
        box.astype(jnp.bfloat16),
    )


def halves(value):
    high = value.astype(jnp.bfloat16)
    return high, (value - high.astype(jnp.float32)).astype(jnp.bfloat16)


def mm(a, b, dims=((1,), (0,))):
    return lax.dot_general(a, b, (dims, ((), ())), preferred_element_type=jnp.float32)


NT = ((1,), (1,))
TN = ((0,), (0,))


def spread_kernel(
    n_chan, n_tm, piece,
    x_hbm, table_hbm, live_hbm, valid_hbm,
    out_hbm,
    live_ref, valid_ref, xpad, tables, mask_rows, turned, send1, recv1, near1, pair, near_pair, cross, near_cross, send2,
    halo_send, halo_recv, local_sem, send1_sem, recv1_sem, near_send, near_recv, send2_sem, recv2_sem,
):
    n = n_chan * n_tm
    span = SEGS * SEG_LEN
    bins = BINS // n
    pieces = bins // piece
    chan, tm = lax.axis_index("chan"), lax.axis_index("tm")
    me = chan * n_tm + tm
    half_a, half_b = n_chan // 2, n_tm // 2

    def wrap(index, count):
        return jnp.where(index >= count, index - count, index)

    def upper(index, half):
        return (index >= half).astype(jnp.int32)

    side = upper(chan, half_a)
    near_chan = chan - side * half_a
    near_me = near_chan * n_tm + tm
    partner = wrap(chan + half_a, n_chan) * n_tm + tm

    def device(a, b):
        return {"chan": a, "tm": b}

    def others(first, count, act):
        def one(t, _):
            i = t + count // 2 - 1
            i = jnp.where(i >= count, i - (count - 1), i)
            for j in range(n_tm):
                act(wrap(first + i, count), wrap(tm + j, n_tm))
            return 0

        lax.fori_loop(1, count, one, 0)
        for j in range(1, n_tm):
            act(first, wrap(tm + j, n_tm))

    live_in = pltpu.make_async_copy(live_hbm, live_ref, local_sem.at[6])
    live_in.start()
    valid_in = pltpu.make_async_copy(valid_hbm, valid_ref, local_sem.at[7])
    valid_in.start()
    load = pltpu.make_async_copy(table_hbm, tables, local_sem.at[1])
    load.start()
    part = 8 * SEG_LEN
    cuts = (part - LANES, 3 * part + LANES)
    fills = [
        pltpu.make_async_copy(
            x_hbm.at[:, pl.ds(low, high - low)], xpad.at[:, pl.ds(LANES + low, high - low)],
            local_sem.at[sem],
        )
        for sem, low, high in ((0, *cuts), (8 + 2 * pieces, cuts[1], span), (9 + 2 * pieces, 0, cuts[0]))
    ]
    for fill in fills:
        fill.start()

    barrier = pltpu.get_barrier_semaphore()

    others(
        chan, n_chan,
        lambda a, b: pl.semaphore_signal(
            barrier, inc=1, device_id=device(a, b), device_id_type=MESH
        ),
    )

    to_left = pltpu.make_async_remote_copy(
        src_ref=x_hbm.at[:, pl.ds(0, LANES)],
        dst_ref=xpad.at[:, pl.ds(LANES + span, LANES)],
        send_sem=halo_send.at[0], recv_sem=halo_recv.at[0],
        device_id={"chan": chan, "tm": jnp.maximum(tm - 1, 0)}, device_id_type=MESH,
    )
    to_right = pltpu.make_async_remote_copy(
        src_ref=x_hbm.at[:, pl.ds(span - LANES, LANES)],
        dst_ref=xpad.at[:, pl.ds(0, LANES)],
        send_sem=halo_send.at[1], recv_sem=halo_recv.at[1],
        device_id={"chan": chan, "tm": jnp.minimum(tm + 1, n_tm - 1)}, device_id_type=MESH,
    )
    has_left, has_right = tm > 0, tm < n_tm - 1

    @pl.when(jnp.logical_not(has_left))
    def _():
        xpad[:, 0:LANES] = jnp.zeros((CHAN_ROWS, LANES), jnp.float32)

    @pl.when(jnp.logical_not(has_right))
    def _():
        xpad[:, LANES + span : 2 * LANES + span] = jnp.zeros((CHAN_ROWS, LANES), jnp.float32)

    live_in.wait()
    valid_in.wait()
    valid = valid_ref[...].astype(jnp.float32).astype(jnp.bfloat16)
    live = live_ref[...].astype(jnp.float32)
    mask_sum = jnp.zeros((SUB, LANES), jnp.float32)
    seg_row = lax.broadcasted_iota(jnp.int32, (SUB, SEGS), 0) * PER_LANE
    seg_col = lax.broadcasted_iota(jnp.int32, (SUB, SEGS), 1)
    chan_row = lax.broadcasted_iota(jnp.int32, (CHAN_ROWS, LANES), 0)
    chan_lane = lax.broadcasted_iota(jnp.int32, (CHAN_ROWS, LANES), 1)
    for q in range(PER_LANE):
        pick = (seg_col == seg_row + q).astype(jnp.float32).astype(jnp.bfloat16)
        place = (chan_lane == chan_row + q * CHAN_ROWS).astype(jnp.float32).astype(jnp.bfloat16)
        picked = (mm(pick, valid, NT) * live).astype(jnp.bfloat16)
        mask_sum = mask_sum + mm(picked, place)
    mask_rows[...] = mask_sum

    row = lax.broadcasted_iota(jnp.int32, (ROWS, 2 * LANES), 0)

    def whiten(m, slot):
        window = jnp.concatenate(
            [
                xpad[:, pl.ds(pl.multiple_of(m * 8 * SEG_LEN + i * SEG_LEN, LANES), 2 * SEG_LEN)]
                for i in range(8)
            ],
            axis=0,
        )
        box = tables[3 * ROWS : 5 * ROWS]
        high, low = halves(jnp.abs(window))
        level = (mm(high, box) + mm(low, box)) * (1.0 / (2 * HALF_WIN + 1))
        normed = window[:, SEG_LEN // 2 : SEG_LEN // 2 + SEG_LEN] / (level + 1e-5)
        high, low = halves(normed)
        fwd_hi = tables[0:ROWS]
        spectrum = mm(fwd_hi, high, NT) + mm(fwd_hi, low, NT) + mm(tables[ROWS : 2 * ROWS], high, NT)
        power = spectrum * spectrum
        high, low = halves(power)
        smooth = tables[2 * ROWS : 3 * ROWS]
        smoothed = (mm(smooth, high) + mm(smooth, low)) * (1.0 / (2 * SMOOTH + 1))
        mean_power = jnp.sum(power, axis=0, keepdims=True) * (1.0 / BINS)
        mask = jnp.concatenate(
            [mask_rows[pl.ds(2 * m, 1), :], mask_rows[pl.ds(2 * m + 1, 1), :]], axis=1
        )
        whitened = spectrum * (mask * lax.rsqrt(smoothed + (0.1 * mean_power + 1e-6)))
        whitened = jnp.where(row == 0, mask, jnp.where(row == 1, 0.0, whitened))
        for u in range(2):
            at = (2 * slot + u) * STRIDE
            turned[at : at + ROWS, :] = whitened[:, u * LANES : (u + 1) * LANES]

    def send(source, target, size, place_out, place_in, out_sem, in_sem, a, b):
        return pltpu.make_async_remote_copy(
            src_ref=source.at[pl.ds(place_out, size)], dst_ref=target.at[pl.ds(place_in, size)],
            send_sem=out_sem, recv_sem=in_sem, device_id=device(a, b), device_id_type=MESH,
        )

    def far(h, a, b, owner):
        return send(
            send1, recv1, bins, h * BINS + (a * n_tm + b) * bins, h * BINS + owner * bins,
            send1_sem.at[h], recv1_sem.at[h * n + owner], a, b,
        )

    def near(h, a, b, owner):
        return send(
            send1, near1, bins, h * BINS + (((1 - side) * half_a + a) * n_tm + b) * bins,
            (h * (n // 2) + owner) * bins,
            near_send.at[h], near_recv.at[h * (n // 2) + owner], side * half_a + a, b,
        )

    def keep_far(h):
        return pltpu.make_async_copy(
            send1.at[pl.ds(h * BINS + me * bins, bins)],
            recv1.at[pl.ds(h * BINS + me * bins, bins)], local_sem.at[2 + h],
        )

    def keep_near(h):
        return pltpu.make_async_copy(
            send1.at[pl.ds(h * BINS + partner * bins, bins)],
            near1.at[pl.ds((h * (n // 2) + near_me) * bins, bins)], local_sem.at[4 + h],
        )

    load.wait()
    fills[0].wait()
    whiten(1, 0)
    whiten(2, 1)
    pl.semaphore_wait(barrier, n - 1)

    @pl.when(has_left)
    def _():
        to_left.start()

    @pl.when(has_right)
    def _():
        to_right.start()

    fills[1].wait()
    fills[2].wait()

    def half(h, _):
        @pl.when(h == 1)
        def _():
            whiten(5, 0)
            whiten(6, 1)

            @pl.when(has_left)
            def _():
                to_left.wait_send()
                to_right.wait_recv()

            @pl.when(has_right)
            def _():
                to_right.wait_send()
                to_left.wait_recv()

        whiten(jnp.where(h == 0, 3, 0), 2)
        whiten(jnp.where(h == 0, 4, 7), 3)

        def turn(step, _):
            for i in range(8):
                f = step * 8 + i
                tile = jnp.concatenate(
                    [turned[pl.ds(2 * f + c, SUB // 2, stride=STRIDE), :] for c in range(2)], axis=0
                )
                send1[h * BINS + f] = tile.astype(jnp.bfloat16)
            return 0

        lax.fori_loop(0, BINS // 8, turn, 0)
        others(chan, n_chan, lambda a, b: far(h, a, b, me).start())
        others(near_chan, half_a, lambda a, b: near(h, a, b, near_me).start())
        keep_far(h).start()
        keep_near(h).start()
        return 0

    lax.fori_loop(0, 2, half, 0)

    lane = lax.broadcasted_iota(jnp.int32, (SUB, LANES), 1)
    low_half = lane < LANES // 2
    even = lax.rem(lane // CHAN_ROWS, 2) == 0
    n_all = n_chan * CHAN_ROWS
    depth = 2 * n_tm * SEGS
    groups = n_chan // PER_LANE

    def swap(first, second, distance, keep):
        return (
            jnp.where(keep, first, pltpu.roll(second, distance, 1)),
            jnp.where(keep, pltpu.roll(first, LANES - distance, 1), second),
        )

    def arrange(tiles, into, width, at, g):
        p0, p2 = swap(tiles[0], tiles[2], 64, low_half)
        p1, p3 = swap(tiles[1], tiles[3], 64, low_half)
        u0, u1 = swap(p0, p1, 32, even)
        u2, u3 = swap(p2, p3, 32, even)
        left = pl.multiple_of(g * LANES, LANES)
        right = pl.multiple_of(width + g * LANES, LANES)
        for q, value in enumerate((u0, u1, u2, u3)):
            rows = pl.ds(pl.multiple_of(at + q * SUB, SUB), SUB)
            other = jnp.concatenate([value[SUB // 2 :], -value[: SUB // 2]], axis=0)
            into[rows, pl.ds(left, LANES)] = value.astype(jnp.bfloat16)
            into[rows, pl.ds(right, LANES)] = other.astype(jnp.bfloat16)

    def gather(h, _):
        keep_far(h).wait()
        keep_near(h).wait()

        def near_group(g, _):
            for b in range(n_tm):
                sources = [(g * PER_LANE + i) * n_tm + b for i in range(PER_LANE)]
                for i, source in enumerate(sources):
                    @pl.when(source != near_me)
                    def _():
                        near(h, g * PER_LANE + i, b, source).wait_recv()

                for f in range(bins):
                    tiles = [
                        near1[(h * (n // 2) + source) * bins + f].astype(jnp.float32)
                        for source in sources
                    ]
                    at = f * depth + (h * n_tm + b) * PER_LANE * SUB
                    arrange(tiles, near_pair, n_half, at, g)
            return 0

        def far_group(j, _):
            g = wrap(side * (groups // 2) + j, groups)
            for b in range(n_tm):
                sources = [(g * PER_LANE + i) * n_tm + b for i in range(PER_LANE)]
                for i, source in enumerate(sources):
                    @pl.when(source != me)
                    def _():
                        far(h, g * PER_LANE + i, b, source).wait_recv()

                for f in range(bins):
                    tiles = [
                        recv1[h * BINS + source * bins + f].astype(jnp.float32)
                        for source in sources
                    ]
                    at = f * depth + (h * n_tm + b) * PER_LANE * SUB
                    arrange(tiles, pair, n_all, at, g)
            return 0

        lax.fori_loop(0, groups, far_group, 0)
        lax.fori_loop(0, groups // 2, near_group, 0)
        return 0

    n_half = n_all // 2
    lax.fori_loop(0, 2, gather, 0)

    paired = upper(tm, half_b) == side
    moved_a, moved_b = wrap(chan + half_a, n_chan), wrap(tm + half_b, n_tm)

    def back(s, a, b):
        slot = a * n_tm + b
        spare = jnp.logical_and(upper(a, half_a) != side, upper(b, half_b) != side)
        to_a = jnp.where(spare, wrap(a + half_a, n_chan), a)
        to_b = jnp.where(spare, wrap(b + half_b, n_tm), b)
        owner = jnp.where(spare, partner, me)
        return send(
            send2, out_hbm, 2 * piece, (slot * bins + s * piece) * 2,
            (owner * bins + s * piece) * 2, send2_sem.at[0], recv2_sem.at[0], to_a, to_b,
        )

    def keep_back(s):
        return pltpu.make_async_copy(
            send2.at[pl.ds((me * bins + s * piece) * 2, 2 * piece)],
            out_hbm.at[pl.ds((me * bins + s * piece) * 2, 2 * piece)], local_sem.at[8 + 2 * s],
        )

    def keep_spare(s):
        slot = moved_a * n_tm + moved_b
        return pltpu.make_async_copy(
            send2.at[pl.ds((slot * bins + s * piece) * 2, 2 * piece)],
            out_hbm.at[pl.ds((partner * bins + s * piece) * 2, 2 * piece)],
            local_sem.at[9 + 2 * s],
        )

    def some_bins(s, _):
        for i in range(piece):
            at = pl.ds(pl.multiple_of((s * piece + i) * depth, depth), depth)
            cross[i] = mm(pair[at, :n_all], pair[at, :], TN)
            near_cross[i] = mm(near_pair[at, :n_half], near_pair[at, :], TN)

        def pack(block, width, i, row, lane_block, owner, slot_a, slot_b):
            f = s * piece + i
            at = pl.multiple_of(row * CHAN_ROWS, CHAN_ROWS)
            tops = []
            for c in range(2):
                lanes = pl.ds(pl.multiple_of(c * width + lane_block * LANES, LANES), LANES)
                top = block[i, pl.ds(at, SUB), lanes]
                bottom = block[i, pl.ds(at + SUB, SUB), lanes]
                tops.append(swap(top, bottom, 64, low_half))
            for e in range(2):
                dest = ((slot_a * n_tm + slot_b + e) * bins + f) * 2
                real = tops[0][e].astype(jnp.bfloat16)
                imag = tops[1][e]
                if i == 0:
                    rest = tops[0][e] - real.astype(jnp.float32)
                    imag = jnp.where(jnp.logical_and(owner == 0, f == 0), rest, imag)
                send2[dest] = real
                send2[dest + 1] = imag.astype(jnp.bfloat16)

        for i in range(piece):
            for k in range(half_a):
                mine, outer = side * half_a + k, (1 - side) * half_a + k
                for p in range(n_tm // 2):
                    pack(cross, n_all, i, mine, p, me, mine, 2 * p)
                for p in range(half_b // 2):
                    inside = side * (half_b // 2) + p
                    pack(cross, n_all, i, outer, inside, me, outer, 2 * inside)
                    pack(
                        near_cross, n_half, i, k, p, partner, outer,
                        (1 - side) * half_b + 2 * p,
                    )

        def one(a, b):
            @pl.when(jnp.logical_not(
                jnp.logical_and(paired, jnp.logical_and(a == moved_a, b == moved_b))
            ))
            def _():
                back(s, a, b).start()

        others(chan, n_chan, one)
        keep_back(s).start()

        @pl.when(paired)
        def _():
            keep_spare(s).start()

        return 0

    lax.fori_loop(0, pieces, some_bins, 0)

    for p in range(pieces):
        keep_back(p).wait()

        @pl.when(paired)
        def _():
            keep_spare(p).wait()

    def all_back(count):
        size = count * 2 * bins
        whole = send(
            send2, out_hbm, size, 0, 0, send2_sem.at[0], recv2_sem.at[0], moved_a, moved_b
        )
        whole.wait_recv()
        whole.wait_send()

    @pl.when(paired)
    def _():
        all_back(n - 2)

    @pl.when(jnp.logical_not(paired))
    def _():
        all_back(n - 1)

    for h in range(2):
        send(
            send1, recv1, (n - 1) * bins, 0, 0, send1_sem.at[h], recv1_sem.at[0], moved_a, moved_b
        ).wait_send()
        send(
            send1, near1, (n // 2 - 1) * bins, 0, 0, near_send.at[h], near_recv.at[0],
            moved_a, moved_b,
        ).wait_send()


def lag_kernel(steps, cross_ref, inverse_ref, out_ref, rows, scale):
    step = pl.program_id(0)

    @pl.when(step == 0)
    def _():
        count = cross_ref[0].astype(jnp.float32) + cross_ref[1].astype(jnp.float32)
        scale[...] = (2.0 / jnp.maximum(count, 1.0)).T

        def turn(block, _):
            for i in range(16):
                r = block * 16 + i
                rows[pl.ds(r, SUB, stride=STRIDE), :] = cross_ref[r].astype(jnp.float32)
            return 0

        lax.fori_loop(0, ROWS // 16, turn, 0)

    column = lax.broadcasted_iota(jnp.int32, (LANES, SUB), 1)
    for i in range(SUB // steps):
        index = step * (SUB // steps) + i
        value = rows[pl.ds(pl.multiple_of(index * STRIDE, 8), ROWS), :].astype(jnp.bfloat16)
        lagged = mm(value, inverse_ref[:ROWS], TN) + mm(value, inverse_ref[ROWS:], TN)
        lagged = lagged * jnp.sum(
            jnp.where(column == index, scale[...], 0.0), axis=1, keepdims=True
        )
        out_ref[0, i] = lagged[: LANES // 2]
        out_ref[1, i] = lagged[LANES // 2 :]


def body(n_chan, n_tm, traces, live_channel, valid_segment):
    forward, inverse, smooth, box = make_tables()
    n = n_chan * n_tm
    n_all = n_chan * CHAN_ROWS
    bins = BINS // n
    piece = 1
    pieces = bins // piece
    span = traces.shape[1]
    tables = np.concatenate([*forward, smooth, box], axis=0)
    inverse = np.concatenate(inverse, axis=0)
    hbm = pl.BlockSpec(memory_space=pltpu.HBM)
    dma = pltpu.SemaphoreType.DMA
    tiles = (ROWS, SUB, LANES)
    crossed = pl.pallas_call(
        functools.partial(spread_kernel, n_chan, n_tm, piece),
        out_shape=jax.ShapeDtypeStruct(tiles, jnp.bfloat16),
        in_specs=[hbm] * 4,
        out_specs=hbm,
        scratch_shapes=[
            pltpu.VMEM((1, CHAN_ROWS), jnp.int32),
            pltpu.VMEM((CHAN_ROWS, SEGS), jnp.int32),
            pltpu.VMEM((CHAN_ROWS, span + 2 * LANES), jnp.float32),
            pltpu.VMEM(tables.shape, jnp.bfloat16),
            pltpu.VMEM((SUB, LANES), jnp.float32),
            pltpu.VMEM((SUB // 2 * STRIDE, LANES), jnp.float32),
            pltpu.VMEM(tiles, jnp.bfloat16),
            pltpu.VMEM(tiles, jnp.bfloat16),
            pltpu.VMEM((BINS, SUB, LANES), jnp.bfloat16),
            pltpu.VMEM((bins * 2 * n_tm * SEGS, 2 * n_all), jnp.bfloat16),
            pltpu.VMEM((bins * 2 * n_tm * SEGS, n_all), jnp.bfloat16),
            pltpu.VMEM((piece, n_all, 2 * n_all), jnp.float32),
            pltpu.VMEM((piece, n_all // 2, n_all), jnp.float32),
            pltpu.VMEM(tiles, jnp.bfloat16),
            dma((2,)), dma((2,)), dma((10 + 2 * pieces,)),
            dma((2,)), dma((2 * n,)), dma((2,)), dma((n,)), dma((1,)), dma((1,)),
        ],
        compiler_params=pltpu.CompilerParams(
            collective_id=0, has_side_effects=True, vmem_limit_bytes=VMEM_LIMIT
        ),
        name="spread",
    )(traces, tables, live_channel.reshape(1, CHAN_ROWS), valid_segment)
    steps = 4
    lagged = pl.pallas_call(
        functools.partial(lag_kernel, steps),
        out_shape=jax.ShapeDtypeStruct((2, SUB, LANES // 2, SEG_LEN), jnp.float32),
        grid=(steps,),
        in_specs=[
            pl.BlockSpec(tiles, lambda i: (0, 0, 0)),
            pl.BlockSpec((2 * ROWS, SEG_LEN), lambda i: (0, 0)),
        ],
        out_specs=pl.BlockSpec((2, SUB // steps, LANES // 2, SEG_LEN), lambda i: (0, i, 0, 0)),
        scratch_shapes=[
            pltpu.VMEM((SUB * STRIDE, LANES), jnp.float32),
            pltpu.VMEM((LANES, SUB), jnp.float32),
        ],
        compiler_params=pltpu.CompilerParams(vmem_limit_bytes=VMEM_LIMIT),
        name="lags",
    )(crossed, inverse)
    return lagged.reshape(CHAN_ROWS, LANES // 2, SEG_LEN)


def solution(mesh):
    n_chan, n_tm = mesh.shape["chan"], mesh.shape["tm"]
    return jax.shard_map(
        functools.partial(body, n_chan, n_tm),
        mesh=mesh,
        in_specs=(P("chan", "tm"), P("chan"), P("chan", "tm")),
        out_specs=P("chan", "tm", None),
        check_vma=False,
    )
```

```python
import functools

import jax
import jax.numpy as jnp
import numpy as np
from jax import lax
from jax.experimental import pallas as pl
from jax.experimental.pallas import tpu as pltpu
from jax.sharding import PartitionSpec as P

SEG_LEN = 256
BINS = 128
HALF_WIN = 64
SMOOTH = 4
ROWS = 2 * BINS
LANES = 128
STRIDE = ROWS + 8
SUB = 16
CHAN_ROWS = 32
SEGS = 64
PER_LANE = LANES // CHAN_ROWS
MESH = pl.DeviceIdType.MESH
VMEM_LIMIT = 63 * 1024 * 1024


def split_table(table):
    high = table.astype(jnp.bfloat16)
    low = (table - high.astype(np.float32)).astype(jnp.bfloat16)
    return high, low


def make_tables():
    row_bin = np.arange(ROWS) // 2
    row_imag = np.arange(ROWS) % 2 == 1
    time = np.arange(SEG_LEN)
    phase = 2.0 * np.pi / SEG_LEN * (row_bin[:, None] * time[None, :] % SEG_LEN)
    forward = np.where(row_imag[:, None], -np.sin(phase), np.cos(phase)).astype(np.float32)
    lag = np.arange(SEG_LEN) - BINS
    back = 2.0 * np.pi / SEG_LEN * (row_bin[:, None] * lag[None, :] % SEG_LEN)
    inverse = np.where(row_imag[:, None], -np.sin(back), np.cos(back))
    inverse = (inverse * (row_bin > 0)[:, None]).astype(np.float32)
    smooth = np.abs(row_bin[:, None] - row_bin[None, :]) <= SMOOTH
    sample_in = np.arange(2 * SEG_LEN)[:, None] - SEG_LEN // 2
    sample_out = np.arange(SEG_LEN)[None, :]
    box = np.abs(sample_in - sample_out) <= HALF_WIN
    return (
        split_table(forward),
        split_table(inverse),
        smooth.astype(jnp.bfloat16),
        box.astype(jnp.bfloat16),
    )


def halves(value):
    high = value.astype(jnp.bfloat16)
    return high, (value - high.astype(jnp.float32)).astype(jnp.bfloat16)


def mm(a, b, dims=((1,), (0,))):
    return lax.dot_general(a, b, (dims, ((), ())), preferred_element_type=jnp.float32)


NT = ((1,), (1,))
TN = ((0,), (0,))


def spread_kernel(
    n_chan, n_tm, piece,
    x_hbm, table_hbm, live_hbm, valid_hbm,
    out_hbm,
    live_ref, valid_ref, xpad, tables, mask_rows, turned, send1, recv1, near1, pair, near_pair, cross, near_cross, send2,
    halo_send, halo_recv, local_sem, send1_sem, recv1_sem, near_send, near_recv, send2_sem, recv2_sem,
):
    n = n_chan * n_tm
    span = SEGS * SEG_LEN
    bins = BINS // n
    pieces = bins // piece
    chan, tm = lax.axis_index("chan"), lax.axis_index("tm")
    me = chan * n_tm + tm
    half_a, half_b = n_chan // 2, n_tm // 2

    def wrap(index, count):
        return jnp.where(index >= count, index - count, index)

    def upper(index, half):
        return (index >= half).astype(jnp.int32)

    side = upper(chan, half_a)
    near_chan = chan - side * half_a
    near_me = near_chan * n_tm + tm
    partner = wrap(chan + half_a, n_chan) * n_tm + tm

    def device(a, b):
        return {"chan": a, "tm": b}

    def others(first, count, act):
        for j in range(1, n_tm):
            act(first, wrap(tm + j, n_tm))

        def one(i, _):
            for j in range(n_tm):
                act(wrap(first + i, count), wrap(tm + j, n_tm))
            return 0

        lax.fori_loop(1, count, one, 0)

    live_in = pltpu.make_async_copy(live_hbm, live_ref, local_sem.at[6])
    live_in.start()
    valid_in = pltpu.make_async_copy(valid_hbm, valid_ref, local_sem.at[7])
    valid_in.start()
    load = pltpu.make_async_copy(table_hbm, tables, local_sem.at[1])
    load.start()
    part = 8 * SEG_LEN
    cuts = (part - LANES, 3 * part + LANES)
    fills = [
        pltpu.make_async_copy(
            x_hbm.at[:, pl.ds(low, high - low)], xpad.at[:, pl.ds(LANES + low, high - low)],
            local_sem.at[sem],
        )
        for sem, low, high in ((0, *cuts), (8 + 2 * pieces, cuts[1], span), (9 + 2 * pieces, 0, cuts[0]))
    ]
    for fill in fills:
        fill.start()

    barrier = pltpu.get_barrier_semaphore()

    others(
        chan, n_chan,
        lambda a, b: pl.semaphore_signal(
            barrier, inc=1, device_id=device(a, b), device_id_type=MESH
        ),
    )

    to_left = pltpu.make_async_remote_copy(
        src_ref=x_hbm.at[:, pl.ds(0, LANES)],
        dst_ref=xpad.at[:, pl.ds(LANES + span, LANES)],
        send_sem=halo_send.at[0], recv_sem=halo_recv.at[0],
        device_id={"chan": chan, "tm": jnp.maximum(tm - 1, 0)}, device_id_type=MESH,
    )
    to_right = pltpu.make_async_remote_copy(
        src_ref=x_hbm.at[:, pl.ds(span - LANES, LANES)],
        dst_ref=xpad.at[:, pl.ds(0, LANES)],
        send_sem=halo_send.at[1], recv_sem=halo_recv.at[1],
        device_id={"chan": chan, "tm": jnp.minimum(tm + 1, n_tm - 1)}, device_id_type=MESH,
    )
    has_left, has_right = tm > 0, tm < n_tm - 1

    @pl.when(jnp.logical_not(has_left))
    def _():
        xpad[:, 0:LANES] = jnp.zeros((CHAN_ROWS, LANES), jnp.float32)

    @pl.when(jnp.logical_not(has_right))
    def _():
        xpad[:, LANES + span : 2 * LANES + span] = jnp.zeros((CHAN_ROWS, LANES), jnp.float32)

    live_in.wait()
    valid_in.wait()
    valid = valid_ref[...].astype(jnp.float32).astype(jnp.bfloat16)
    live = live_ref[...].astype(jnp.float32)
    mask_sum = jnp.zeros((SUB, LANES), jnp.float32)
    seg_row = lax.broadcasted_iota(jnp.int32, (SUB, SEGS), 0) * PER_LANE
    seg_col = lax.broadcasted_iota(jnp.int32, (SUB, SEGS), 1)
    chan_row = lax.broadcasted_iota(jnp.int32, (CHAN_ROWS, LANES), 0)
    chan_lane = lax.broadcasted_iota(jnp.int32, (CHAN_ROWS, LANES), 1)
    for q in range(PER_LANE):
        pick = (seg_col == seg_row + q).astype(jnp.float32).astype(jnp.bfloat16)
        place = (chan_lane == chan_row + q * CHAN_ROWS).astype(jnp.float32).astype(jnp.bfloat16)
        picked = (mm(pick, valid, NT) * live).astype(jnp.bfloat16)
        mask_sum = mask_sum + mm(picked, place)
    mask_rows[...] = mask_sum

    row = lax.broadcasted_iota(jnp.int32, (ROWS, 2 * LANES), 0)

    def whiten(m, slot):
        window = jnp.concatenate(
            [
                xpad[:, pl.ds(pl.multiple_of(m * 8 * SEG_LEN + i * SEG_LEN, LANES), 2 * SEG_LEN)]
                for i in range(8)
            ],
            axis=0,
        )
        box = tables[3 * ROWS : 5 * ROWS]
        high, low = halves(jnp.abs(window))
        level = (mm(high, box) + mm(low, box)) * (1.0 / (2 * HALF_WIN + 1))
        normed = window[:, SEG_LEN // 2 : SEG_LEN // 2 + SEG_LEN] / (level + 1e-5)
        high, low = halves(normed)
        fwd_hi = tables[0:ROWS]
        spectrum = mm(fwd_hi, high, NT) + mm(fwd_hi, low, NT) + mm(tables[ROWS : 2 * ROWS], high, NT)
        power = spectrum * spectrum
        high, low = halves(power)
        smooth = tables[2 * ROWS : 3 * ROWS]
        smoothed = (mm(smooth, high) + mm(smooth, low)) * (1.0 / (2 * SMOOTH + 1))
        mean_power = jnp.sum(power, axis=0, keepdims=True) * (1.0 / BINS)
        mask = jnp.concatenate(
            [mask_rows[pl.ds(2 * m, 1), :], mask_rows[pl.ds(2 * m + 1, 1), :]], axis=1
        )
        whitened = spectrum * (mask * lax.rsqrt(smoothed + (0.1 * mean_power + 1e-6)))
        whitened = jnp.where(row == 0, mask, jnp.where(row == 1, 0.0, whitened))
        for u in range(2):
            at = (2 * slot + u) * STRIDE
            turned[at : at + ROWS, :] = whitened[:, u * LANES : (u + 1) * LANES]

    def send(source, target, size, place_out, place_in, out_sem, in_sem, a, b):
        return pltpu.make_async_remote_copy(
            src_ref=source.at[pl.ds(place_out, size)], dst_ref=target.at[pl.ds(place_in, size)],
            send_sem=out_sem, recv_sem=in_sem, device_id=device(a, b), device_id_type=MESH,
        )

    def far(h, a, b, owner):
        return send(
            send1, recv1, bins, h * BINS + (a * n_tm + b) * bins, h * BINS + owner * bins,
            send1_sem.at[h], recv1_sem.at[h * n + owner], a, b,
        )

    def near(h, a, b, owner):
        return send(
            send1, near1, bins, h * BINS + (((1 - side) * half_a + a) * n_tm + b) * bins,
            (h * (n // 2) + owner) * bins,
            near_send.at[h], near_recv.at[h * (n // 2) + owner], side * half_a + a, b,
        )

    def keep_far(h):
        return pltpu.make_async_copy(
            send1.at[pl.ds(h * BINS + me * bins, bins)],
            recv1.at[pl.ds(h * BINS + me * bins, bins)], local_sem.at[2 + h],
        )

    def keep_near(h):
        return pltpu.make_async_copy(
            send1.at[pl.ds(h * BINS + partner * bins, bins)],
            near1.at[pl.ds((h * (n // 2) + near_me) * bins, bins)], local_sem.at[4 + h],
        )

    load.wait()
    fills[0].wait()
    whiten(1, 0)
    whiten(2, 1)
    pl.semaphore_wait(barrier, n - 1)

    @pl.when(has_left)
    def _():
        to_left.start()

    @pl.when(has_right)
    def _():
        to_right.start()

    fills[1].wait()
    fills[2].wait()

    def half(h, _):
        @pl.when(h == 1)
        def _():
            whiten(5, 0)
            whiten(6, 1)

            @pl.when(has_left)
            def _():
                to_left.wait_send()
                to_right.wait_recv()

            @pl.when(has_right)
            def _():
                to_right.wait_send()
                to_left.wait_recv()

        whiten(jnp.where(h == 0, 3, 0), 2)
        whiten(jnp.where(h == 0, 4, 7), 3)

        def turn(step, _):
            for i in range(8):
                f = step * 8 + i
                tile = jnp.concatenate(
                    [turned[pl.ds(2 * f + c, SUB // 2, stride=STRIDE), :] for c in range(2)], axis=0
                )
                send1[h * BINS + f] = tile.astype(jnp.bfloat16)
            return 0

        lax.fori_loop(0, BINS // 8, turn, 0)
        others(chan, n_chan, lambda a, b: far(h, a, b, me).start())
        others(near_chan, half_a, lambda a, b: near(h, a, b, near_me).start())
        keep_far(h).start()
        keep_near(h).start()
        return 0

    lax.fori_loop(0, 2, half, 0)

    lane = lax.broadcasted_iota(jnp.int32, (SUB, LANES), 1)
    low_half = lane < LANES // 2
    even = lax.rem(lane // CHAN_ROWS, 2) == 0
    n_all = n_chan * CHAN_ROWS
    depth = 2 * n_tm * SEGS
    groups = n_chan // PER_LANE

    def swap(first, second, distance, keep):
        return (
            jnp.where(keep, first, pltpu.roll(second, distance, 1)),
            jnp.where(keep, pltpu.roll(first, LANES - distance, 1), second),
        )

    def arrange(tiles, into, width, at, g):
        p0, p2 = swap(tiles[0], tiles[2], 64, low_half)
        p1, p3 = swap(tiles[1], tiles[3], 64, low_half)
        u0, u1 = swap(p0, p1, 32, even)
        u2, u3 = swap(p2, p3, 32, even)
        left = pl.multiple_of(g * LANES, LANES)
        right = pl.multiple_of(width + g * LANES, LANES)
        for q, value in enumerate((u0, u1, u2, u3)):
            rows = pl.ds(pl.multiple_of(at + q * SUB, SUB), SUB)
            other = jnp.concatenate([value[SUB // 2 :], -value[: SUB // 2]], axis=0)
            into[rows, pl.ds(left, LANES)] = value.astype(jnp.bfloat16)
            into[rows, pl.ds(right, LANES)] = other.astype(jnp.bfloat16)

    def gather(h, _):
        keep_far(h).wait()
        keep_near(h).wait()

        def near_group(g, _):
            for b in range(n_tm):
                sources = [(g * PER_LANE + i) * n_tm + b for i in range(PER_LANE)]
                for i, source in enumerate(sources):
                    @pl.when(source != near_me)
                    def _():
                        near(h, g * PER_LANE + i, b, source).wait_recv()

                for f in range(bins):
                    tiles = [
                        near1[(h * (n // 2) + source) * bins + f].astype(jnp.float32)
                        for source in sources
                    ]
                    at = f * depth + (h * n_tm + b) * PER_LANE * SUB
                    arrange(tiles, near_pair, n_half, at, g)
            return 0

        def far_group(j, _):
            g = wrap(side * (groups // 2) + j, groups)
            for b in range(n_tm):
                sources = [(g * PER_LANE + i) * n_tm + b for i in range(PER_LANE)]
                for i, source in enumerate(sources):
                    @pl.when(source != me)
                    def _():
                        far(h, g * PER_LANE + i, b, source).wait_recv()

                for f in range(bins):
                    tiles = [
                        recv1[h * BINS + source * bins + f].astype(jnp.float32)
                        for source in sources
                    ]
                    at = f * depth + (h * n_tm + b) * PER_LANE * SUB
                    arrange(tiles, pair, n_all, at, g)
            return 0

        lax.fori_loop(0, groups, far_group, 0)
        lax.fori_loop(0, groups // 2, near_group, 0)
        return 0

    n_half = n_all // 2
    lax.fori_loop(0, 2, gather, 0)

    paired = upper(tm, half_b) == side
    moved_a, moved_b = wrap(chan + half_a, n_chan), wrap(tm + half_b, n_tm)

    def back(s, a, b):
        slot = a * n_tm + b
        spare = jnp.logical_and(upper(a, half_a) != side, upper(b, half_b) != side)
        to_a = jnp.where(spare, wrap(a + half_a, n_chan), a)
        to_b = jnp.where(spare, wrap(b + half_b, n_tm), b)
        owner = jnp.where(spare, partner, me)
        return send(
            send2, out_hbm, 2 * piece, (slot * bins + s * piece) * 2,
            (owner * bins + s * piece) * 2, send2_sem.at[0], recv2_sem.at[0], to_a, to_b,
        )

    def keep_back(s):
        return pltpu.make_async_copy(
            send2.at[pl.ds((me * bins + s * piece) * 2, 2 * piece)],
            out_hbm.at[pl.ds((me * bins + s * piece) * 2, 2 * piece)], local_sem.at[8 + 2 * s],
        )

    def keep_spare(s):
        slot = moved_a * n_tm + moved_b
        return pltpu.make_async_copy(
            send2.at[pl.ds((slot * bins + s * piece) * 2, 2 * piece)],
            out_hbm.at[pl.ds((partner * bins + s * piece) * 2, 2 * piece)],
            local_sem.at[9 + 2 * s],
        )

    def some_bins(s, _):
        for i in range(piece):
            at = pl.ds(pl.multiple_of((s * piece + i) * depth, depth), depth)
            cross[i] = mm(pair[at, :n_all], pair[at, :], TN)
            near_cross[i] = mm(near_pair[at, :n_half], near_pair[at, :], TN)

        def pack(block, width, i, row, lane_block, owner, slot_a, slot_b):
            f = s * piece + i
            at = pl.multiple_of(row * CHAN_ROWS, CHAN_ROWS)
            tops = []
            for c in range(2):
                lanes = pl.ds(pl.multiple_of(c * width + lane_block * LANES, LANES), LANES)
                top = block[i, pl.ds(at, SUB), lanes]
                bottom = block[i, pl.ds(at + SUB, SUB), lanes]
                tops.append(swap(top, bottom, 64, low_half))
            for e in range(2):
                dest = ((slot_a * n_tm + slot_b + e) * bins + f) * 2
                real = tops[0][e].astype(jnp.bfloat16)
                imag = tops[1][e]
                if i == 0:
                    rest = tops[0][e] - real.astype(jnp.float32)
                    imag = jnp.where(jnp.logical_and(owner == 0, f == 0), rest, imag)
                send2[dest] = real
                send2[dest + 1] = imag.astype(jnp.bfloat16)

        for i in range(piece):
            for k in range(half_a):
                mine, outer = side * half_a + k, (1 - side) * half_a + k
                for p in range(n_tm // 2):
                    pack(cross, n_all, i, mine, p, me, mine, 2 * p)
                for p in range(half_b // 2):
                    inside = side * (half_b // 2) + p
                    pack(cross, n_all, i, outer, inside, me, outer, 2 * inside)
                    pack(
                        near_cross, n_half, i, k, p, partner, outer,
                        (1 - side) * half_b + 2 * p,
                    )

        def one(a, b):
            @pl.when(jnp.logical_not(
                jnp.logical_and(paired, jnp.logical_and(a == moved_a, b == moved_b))
            ))
            def _():
                back(s, a, b).start()

        others(chan, n_chan, one)
        keep_back(s).start()

        @pl.when(paired)
        def _():
            keep_spare(s).start()

        return 0

    lax.fori_loop(0, pieces, some_bins, 0)

    for p in range(pieces):
        keep_back(p).wait()

        @pl.when(paired)
        def _():
            keep_spare(p).wait()

    def all_back(count):
        size = count * 2 * bins
        whole = send(
            send2, out_hbm, size, 0, 0, send2_sem.at[0], recv2_sem.at[0], moved_a, moved_b
        )
        whole.wait_recv()
        whole.wait_send()

    @pl.when(paired)
    def _():
        all_back(n - 2)

    @pl.when(jnp.logical_not(paired))
    def _():
        all_back(n - 1)

    for h in range(2):
        send(
            send1, recv1, (n - 1) * bins, 0, 0, send1_sem.at[h], recv1_sem.at[0], moved_a, moved_b
        ).wait_send()
        send(
            send1, near1, (n // 2 - 1) * bins, 0, 0, near_send.at[h], near_recv.at[0],
            moved_a, moved_b,
        ).wait_send()


def lag_kernel(steps, cross_hbm, inverse_ref, out_ref, cross_ref, rows, scale, sems):
    step = pl.program_id(0)

    @pl.when(step == 0)
    def _():
        size = ROWS // 4
        copies = [
            pltpu.make_async_copy(
                cross_hbm.at[pl.ds(k * size, size)], cross_ref.at[pl.ds(k * size, size)], sems.at[k]
            )
            for k in range(4)
        ]
        for copy in copies:
            copy.start()
        copies[0].wait()
        count = cross_ref[0].astype(jnp.float32) + cross_ref[1].astype(jnp.float32)
        scale[...] = (2.0 / jnp.maximum(count, 1.0)).T

        def turn(block, _):
            for i in range(16):
                r = block * 16 + i
                rows[pl.ds(r, SUB, stride=STRIDE), :] = cross_ref[r].astype(jnp.float32)
            return 0

        for k in range(4):
            if k > 0:
                copies[k].wait()
            lax.fori_loop(k * size // 16, (k + 1) * size // 16, turn, 0)

    column = lax.broadcasted_iota(jnp.int32, (LANES, SUB), 1)
    for i in range(SUB // steps):
        index = step * (SUB // steps) + i
        value = rows[pl.ds(pl.multiple_of(index * STRIDE, 8), ROWS), :].astype(jnp.bfloat16)
        lagged = mm(value, inverse_ref[:ROWS], TN) + mm(value, inverse_ref[ROWS:], TN)
        lagged = lagged * jnp.sum(
            jnp.where(column == index, scale[...], 0.0), axis=1, keepdims=True
        )
        out_ref[0, i] = lagged[: LANES // 2]
        out_ref[1, i] = lagged[LANES // 2 :]


def body(n_chan, n_tm, traces, live_channel, valid_segment):
    forward, inverse, smooth, box = make_tables()
    n = n_chan * n_tm
    n_all = n_chan * CHAN_ROWS
    bins = BINS // n
    piece = 1
    pieces = bins // piece
    span = traces.shape[1]
    tables = np.concatenate([*forward, smooth, box], axis=0)
    inverse = np.concatenate(inverse, axis=0)
    hbm = pl.BlockSpec(memory_space=pltpu.HBM)
    dma = pltpu.SemaphoreType.DMA
    tiles = (ROWS, SUB, LANES)
    crossed = pl.pallas_call(
        functools.partial(spread_kernel, n_chan, n_tm, piece),
        out_shape=jax.ShapeDtypeStruct(tiles, jnp.bfloat16),
        in_specs=[hbm] * 4,
        out_specs=hbm,
        scratch_shapes=[
            pltpu.VMEM((1, CHAN_ROWS), jnp.int32),
            pltpu.VMEM((CHAN_ROWS, SEGS), jnp.int32),
            pltpu.VMEM((CHAN_ROWS, span + 2 * LANES), jnp.float32),
            pltpu.VMEM(tables.shape, jnp.bfloat16),
            pltpu.VMEM((SUB, LANES), jnp.float32),
            pltpu.VMEM((SUB // 2 * STRIDE, LANES), jnp.float32),
            pltpu.VMEM(tiles, jnp.bfloat16),
            pltpu.VMEM(tiles, jnp.bfloat16),
            pltpu.VMEM((BINS, SUB, LANES), jnp.bfloat16),
            pltpu.VMEM((bins * 2 * n_tm * SEGS, 2 * n_all), jnp.bfloat16),
            pltpu.VMEM((bins * 2 * n_tm * SEGS, n_all), jnp.bfloat16),
            pltpu.VMEM((piece, n_all, 2 * n_all), jnp.float32),
            pltpu.VMEM((piece, n_all // 2, n_all), jnp.float32),
            pltpu.VMEM(tiles, jnp.bfloat16),
            dma((2,)), dma((2,)), dma((10 + 2 * pieces,)),
            dma((2,)), dma((2 * n,)), dma((2,)), dma((n,)), dma((1,)), dma((1,)),
        ],
        compiler_params=pltpu.CompilerParams(
            collective_id=0, has_side_effects=True, vmem_limit_bytes=VMEM_LIMIT
        ),
        name="spread",
    )(traces, tables, live_channel.reshape(1, CHAN_ROWS), valid_segment)
    steps = 4
    lagged = pl.pallas_call(
        functools.partial(lag_kernel, steps),
        out_shape=jax.ShapeDtypeStruct((2, SUB, LANES // 2, SEG_LEN), jnp.float32),
        grid=(steps,),
        in_specs=[
            hbm,
            pl.BlockSpec((2 * ROWS, SEG_LEN), lambda i: (0, 0)),
        ],
        out_specs=pl.BlockSpec((2, SUB // steps, LANES // 2, SEG_LEN), lambda i: (0, i, 0, 0)),
        scratch_shapes=[
            pltpu.VMEM(tiles, jnp.bfloat16),
            pltpu.VMEM((SUB * STRIDE, LANES), jnp.float32),
            pltpu.VMEM((LANES, SUB), jnp.float32),
            dma((4,)),
        ],
        compiler_params=pltpu.CompilerParams(vmem_limit_bytes=VMEM_LIMIT),
        name="lags",
    )(crossed, inverse)
    return lagged.reshape(CHAN_ROWS, LANES // 2, SEG_LEN)


def solution(mesh):
    n_chan, n_tm = mesh.shape["chan"], mesh.shape["tm"]
    return jax.shard_map(
        functools.partial(body, n_chan, n_tm),
        mesh=mesh,
        in_specs=(P("chan", "tm"), P("chan"), P("chan", "tm")),
        out_specs=P("chan", "tm", None),
        check_vma=False,
    )
```
